512 devices in a mesh: kv: 64 (over y, z), tp: 8 (over x, core).
Axes of the slice: x: 4, y: 8, z: 8, core: 2. Of those that a mesh axis runs over, the one named last changes fastest.
Arguments:
- queries: bfloat16 [1024, 2048], P('kv', 'tp'), may hold values from -6 to 6
- prefix_ids: int32 [1024, 1], P('kv'), may hold values from 0 to 7, as said below
- prefix_kv: bfloat16 [2, 131072, 1024], P(None, 'kv', 'tp'), may hold values from -6 to 6
- prefix_scales: float32 [2, 8, 131072], P(None, 'tp', 'kv'), may hold values from 0.5 to 2
- suffix_kv: bfloat16 [2, 1024, 128, 1024], P(None, 'kv', None, 'tp'), may hold values from -9 to 9
- suffix_lengths: int32 [1024], P('kv'), may hold values from 1 to 128
- out_weight: bfloat16 [2048, 4608], P('tp'), may hold values from -1.41421356 to 1.41421356
- residual: bfloat16 [1024, 4608], P('kv', 'tp'), may hold values from -6 to 6
- norm_gain: float32 [4608], P('tp'), may hold values from 0.1 to 1.9
Outputs:
- mixed: bfloat16 [1024, 4608], P('kv', 'tp')
The draws below stay inside these ranges and needn't reach their ends.
Inputs may be any that keep to these rules, and one draw needn't show every extreme that they name: `prefix_ids`: among the 16 requests of one index of kv at most 6 have any one prefix; in every draw one prefix has exactly 6 requests on every index of kv.
All inputs are finite; a program needn't handle non-finite values.
Results may differ from the reference program's by a relative error of at most 0.0049.
Values may be sent and summed in bfloat16 or wider, within the bound.
A program may use at most 64 MiB of HBM per device.

```python
import math
import jax
import jax.numpy as jnp
from jax import lax

D = 4608
H = 16
KVH = 8
HD = 128
NPRE = 8
R_DEV = 16
SUF = 128
CAP = 6
REQUESTS = 1024
PRE_LEN = 16384
PRE_ALL = 131072


def draw_prefix_ids(key, part):
    key = jax.random.fold_in(key, 7)
    busiest = jax.random.randint(jax.random.fold_in(key, 1), (), 0, NPRE, dtype=jnp.int32)
    slot_pool = jnp.arange((NPRE - 1) * CAP, dtype=jnp.int32) // CAP

    def one_block(block_key):
        pick_key, order_key = jax.random.split(block_key)
        chosen = slot_pool[jax.random.permutation(pick_key, (NPRE - 1) * CAP)[:R_DEV - CAP]]
        others = (busiest + 1 + chosen) % NPRE
        block_ids = jnp.concatenate([jnp.full((CAP,), busiest, dtype=jnp.int32), others])
        return block_ids[jax.random.permutation(order_key, R_DEV)]
    block_keys = jax.random.split(jax.random.fold_in(key, 2), REQUESTS // R_DEV)
    return jax.vmap(one_block)(block_keys).reshape(REQUESTS, 1).astype(jnp.int32)


def draw_suffix_lengths(key, part):
    key = jax.random.fold_in(key, 5)
    length_key, place_key = jax.random.split(key)
    lengths = jax.random.randint(length_key, (REQUESTS,), 1, SUF + 1, dtype=jnp.int32)
    fullest = jax.random.randint(place_key, (), 0, REQUESTS, dtype=jnp.int32)
    return jnp.where(jnp.arange(REQUESTS, dtype=jnp.int32) == fullest, SUF, lengths).astype(jnp.int32)


def draw_out_weight(key, part):
    key = jax.random.fold_in(key, 11)
    base_key, column_key = jax.random.split(key)
    position = jnp.arange(D, dtype=jnp.float32) / D
    spread_draw = jax.random.uniform(column_key, (D,), jnp.float32) - 0.5
    base = jnp.clip(jax.random.normal(base_key, (H * HD, D), jnp.float32), -6.0, 6.0)
    column_scale = jnp.exp(jnp.log(3.0) * position + jnp.log(10.0) * spread_draw)
    return (base * (H * HD) ** (-0.5) * column_scale[None, :]).astype(jnp.bfloat16)


def block_scale(stream_key, shape, shards, least, largest):
    loudness = 1.0
    for dim, blocks in shards:
        draws = jax.random.uniform(jax.random.fold_in(jax.random.fold_in(stream_key, 6), dim), (blocks,), jnp.float32, least / len(shards), largest / len(shards))
        loudness = loudness * jnp.repeat(jnp.exp(draws), shape[dim] // blocks).reshape((-1,) + (1,) * (len(shape) - 1 - dim))
    return loudness


def centred(stream_key, extent, width, bound, cuts=(), kind=jnp.bfloat16):
    gain = block_scale(stream_key, extent, cuts, -0.22, 0.18) if cuts else 1.0
    array = jax.random.normal(stream_key, extent, jnp.float32) * width * gain
    return jnp.minimum(jnp.maximum(array, -bound), bound).astype(kind)


def setup_inputs(seed: int = 0) -> dict:
    arg_keys = jax.random.split(jax.random.key(seed), 10)
    queries = centred(arg_keys[0], (REQUESTS, H * HD), 1.0, 6.0, ((0, 64), (1, 8)))
    prefix_ids = draw_prefix_ids(jax.random.fold_in(arg_keys[9], 71), 0)
    prefix_kv = centred(arg_keys[2], (2, PRE_ALL, KVH * HD), 1.0, 6.0, ((1, 64), (2, 8)))
    prefix_scales = jnp.clip(jnp.exp(math.log(2.0) - 1.3862944 * jax.random.uniform(arg_keys[3], (2, KVH, PRE_ALL), jnp.float32) ** block_scale(arg_keys[3], (2, KVH, PRE_ALL), ((1, 8), (2, 64)), -0.2, 0.2)), 0.5, 2.0)
    suffix_kv = centred(arg_keys[4], (2, REQUESTS, SUF, KVH * HD), 1.5, 9.0, ((1, 64), (3, 8)))
    suffix_lengths = draw_suffix_lengths(jax.random.fold_in(arg_keys[9], 71), 0)
    out_weight = draw_out_weight(jax.random.fold_in(arg_keys[9], 71), 0)
    residual = centred(arg_keys[7], (REQUESTS, D), 1.0, 6.0, ((0, 64), (1, 8)))
    norm_gain = jnp.clip(1.0 + 0.18 * jax.random.normal(arg_keys[8], (D,), jnp.float32), 0.1, 1.9)
    return {"queries": queries, "prefix_ids": prefix_ids, "prefix_kv": prefix_kv, "prefix_scales": prefix_scales, "suffix_kv": suffix_kv, "suffix_lengths": suffix_lengths, "out_weight": out_weight, "residual": residual, "norm_gain": norm_gain}


score_scale = 144.0 ** (-0.5)

def capped(raw_scores):
    return 50.0 * jnp.tanh(raw_scores / 50.0)

def reference(queries, prefix_ids, prefix_kv, prefix_scales, suffix_kv, suffix_lengths, out_weight, residual, norm_gain):
    group_size = H // KVH

    def one_request(index):
        query_row = queries[index]
        start = prefix_ids[index, 0].astype(jnp.int32) * PRE_LEN
        zero = jnp.int32(0)
        cache_block = lax.dynamic_slice(prefix_kv, (zero, start, zero), (2, PRE_LEN, KVH * HD))
        scale_block = lax.dynamic_slice(prefix_scales, (zero, zero, start), (2, KVH, PRE_LEN))
        own_cache = lax.dynamic_slice(suffix_kv, (zero, index.astype(jnp.int32), zero, zero), (2, 1, SUF, KVH * HD))[:, 0]
        live = jnp.arange(SUF, dtype=jnp.int32) < suffix_lengths[index]
        pieces = []
        for head_index in range(KVH):
            head_rows = query_row[head_index * group_size * HD:(head_index + 1) * group_size * HD].reshape(group_size, HD)
            columns = slice(head_index * HD, (head_index + 1) * HD)
            raw_scores = jnp.dot(head_rows, cache_block[0, :, columns].T, preferred_element_type=jnp.float32)
            scores = capped(raw_scores * scale_block[0, head_index][None, :] * score_scale)
            exponent = jnp.exp(scores)
            pre_total = lax.optimization_barrier(jnp.sum(exponent, axis=1))
            weights = (exponent * scale_block[1, head_index][None, :]).astype(jnp.bfloat16)
            pre_out = jnp.dot(weights, cache_block[1, :, columns], preferred_element_type=jnp.float32)
            raw_suffix = jnp.dot(head_rows, own_cache[0, :, columns].T, preferred_element_type=jnp.float32)
            suffix_scores = capped(raw_suffix * score_scale)
            suffix_exp = jnp.where(live[None, :], jnp.exp(suffix_scores), jnp.float32(0.0))
            suf_total = lax.optimization_barrier(jnp.sum(suffix_exp, axis=1))
            suf_out = jnp.dot(suffix_exp.astype(jnp.bfloat16), own_cache[1, :, columns], preferred_element_type=jnp.float32)
            merged = (pre_out + suf_out) / (pre_total + suf_total)[:, None]
            pieces.append(merged.astype(jnp.bfloat16).reshape(group_size * HD))
        return jnp.concatenate(pieces)
    attention = lax.map(one_request, jnp.arange(REQUESTS, dtype=jnp.int32))
    projection = jnp.dot(attention, out_weight, preferred_element_type=jnp.float32)
    mean_square = lax.optimization_barrier(jnp.mean(projection * projection, axis=1))
    normed = projection * lax.rsqrt(mean_square + 1e-06)[:, None] * norm_gain[None, :]
    return (residual.astype(jnp.float32) + normed).astype(jnp.bfloat16)
```

```python
import jax
import jax.numpy as jnp
from jax import lax
from jax.experimental import pallas as pl
from jax.experimental.pallas import tpu as pltpu
from jax.sharding import PartitionSpec as P

HD = 128
NPRE = 8
SLOTS = 6
SLAB = 16
MESH = pl.DeviceIdType.MESH
BF = jnp.bfloat16
F32 = jnp.float32
LOG2E = 1.4426950408889634
SCORE = 144.0 ** (-0.5)
CHUNK = 256


def iota(shape, dim):
    return lax.broadcasted_iota(jnp.int32, shape, dim)


def nt(a, b):
    return lax.dot_general(a, b, (((1,), (1,)), ((), ())), preferred_element_type=F32)


def mm(a, b):
    return jnp.dot(a, b, preferred_element_type=F32)


def split(a):
    high = a.astype(BF)
    return high, (a - high.astype(F32)).astype(BF)


def kernel(
    nz, ny, nx,
    q_ref, ids_ref, kv_ref, scales_ref, suf_ref, len_ref, w_ref, res_ref, gain_ref,
    o_ref,
    q_v, kv_v, sc_v, suf_v, w_v, res_v, gain_v,
    slots, gathered, blocks, msgs, back, part, parts, square, squares, out_v,
    local_sem, go_y, go_z, sy, ry, sz, rz, sr, rr, sx, rx, ss, rs,
):
    kv, tp = lax.axis_index("kv"), lax.axis_index("tp")
    y, z = lax.div(kv, nz), lax.rem(kv, nz)
    x, core = lax.div(tp, 2), lax.rem(tp, 2)

    barrier = pltpu.get_barrier_semaphore()

    def here(to_kv, to_tp):
        pl.semaphore_signal(barrier, inc=1, device_id=(to_kv, to_tp), device_id_type=MESH)

    here(kv, x * 2 + (1 - core))
    for i in (4, 3, 5, 2, 6, 1, 7):
        here(y * nz + lax.rem(z + i, nz), x * 2 + 1)
    for i in (4, 3, 5, 2, 6, 1, 7):
        here(lax.rem(y + i, ny) * nz + z, x * 2)
    for i in (2, 1, 3):
        here(kv, lax.rem(x + i, nx) * 2 + 1)

    def fetch(i, src, dst):
        c = pltpu.make_async_copy(src, dst, local_sem.at[i])
        c.start()
        return c

    got_q = fetch(0, q_ref, q_v)
    got_kv = fetch(1, kv_ref, kv_v)
    got_sc = fetch(2, scales_ref, sc_v)
    got_suf = fetch(3, suf_ref, suf_v)
    got_w = fetch(4, w_ref, w_v)
    got_res = fetch(5, res_ref, res_v)
    got_gain = fetch(6, gain_ref, gain_v)

    row16, lane16 = iota((16, 128), 0), iota((16, 128), 1)
    ids_row = ids_ref[...].astype(F32)
    square16 = iota((16, 16), 0), iota((16, 16), 1)
    ids = jnp.sum(jnp.where(square16[0] == square16[1], ids_row, 0.0), axis=1, keepdims=True)
    same = jnp.where(ids == ids_row, 1.0, 0.0)
    rank = jnp.sum(jnp.where(square16[1] < square16[0], same, 0.0), axis=1, keepdims=True)
    rank_row = jnp.sum(jnp.where(square16[0] < square16[1], same, 0.0), axis=0, keepdims=True)
    place = (ids * SLAB + rank).astype(jnp.int32)
    place_row = (ids_row * SLAB + rank_row).astype(jnp.int32)

    got_q.wait()
    row128 = iota((128, 16), 0)
    picks = [jnp.where(row128 == place_row + h * SLOTS, 1.0, 0.0).astype(BF) for h in range(2)]
    slotted = mm(picks[0], q_v[:, :HD]) + mm(picks[1], q_v[:, HD:])
    slots[...] = slotted.astype(BF).reshape(NPRE, SLAB, HD)

    @pl.when(core == 0)
    def _():
        pl.semaphore_wait(barrier, 2 * (ny - 1) + 1)
        pl.semaphore_signal(go_y, inc=1, device_id=(kv, tp + 1), device_id_type=MESH)

    @pl.when(core == 1)
    def _():
        pl.semaphore_wait(go_y, 1)

    def to_holder(i):
        p = lax.rem(y + i, ny)
        return pltpu.make_async_remote_copy(
            src_ref=slots.at[p], dst_ref=gathered.at[y], send_sem=sy.at[i], recv_sem=ry.at[y],
            device_id=(p * nz + z, tp), device_id_type=MESH,
        )

    for i in (4, 3, 5, 2, 6, 1, 7):
        to_holder(i).start()
    gathered[y] = slots[y]

    got_suf.wait()
    eye = jnp.where(iota((32, 16), 1) == lax.rem(iota((32, 16), 0), 16), 1.0, 0.0)
    lens = jnp.sum(eye * len_ref[...].astype(F32), axis=1, keepdims=True).astype(jnp.int32)
    own_q = jnp.concatenate([q_v[:, :HD], q_v[:, HD:]], axis=0)
    own_request = lax.rem(iota((32, CHUNK), 0), 16)
    suf_out = jnp.zeros((32, HD), F32)
    suf_total = jnp.zeros((32, 128), F32)
    for c in range(8):
        k = suf_v[0, 2 * c : 2 * c + 2].reshape(CHUNK, HD)
        v = suf_v[1, 2 * c : 2 * c + 2].reshape(CHUNK, HD)
        e = jnp.exp2(jnp.tanh(nt(own_q, k) * (SCORE / 50.0)) * (50.0 * LOG2E))
        at = iota((32, CHUNK), 1)
        live = (lax.div(at, 128) + 2 * c == own_request) & (lax.rem(at, 128) < lens)
        e = jnp.where(live, e, 0.0)
        suf_total += e[:, :128] + e[:, 128:]
        suf_out += mm(e.astype(BF), v)
    suf_total = jnp.sum(suf_total, axis=1, keepdims=True)

    got_kv.wait()
    got_sc.wait()
    sc_v[0] = sc_v[0] * (SCORE / 50.0)

    def from_source(i):
        return pltpu.make_async_remote_copy(
            src_ref=slots.at[i], dst_ref=gathered.at[i], send_sem=sy.at[i], recv_sem=ry.at[i],
            device_id=(kv, tp), device_id_type=MESH,
        )

    for i in range(1, ny):
        from_source(lax.rem(y + i, ny)).wait_recv()
    compact = jnp.where(
        iota((96, 128), 1) == lax.div(iota((96, 128), 0), 12) * SLAB + lax.rem(iota((96, 128), 0), 12), 1.0, 0.0
    ).astype(BF)
    blocks[z] = mm(compact, gathered[...].reshape(128, HD)).astype(BF)

    @pl.when(core == 1)
    def _():
        pl.semaphore_wait(barrier, 2 * (nz - 1) + 1 + 2 * (nx - 1))
        pl.semaphore_signal(go_z, inc=1, device_id=(kv, tp - 1), device_id_type=MESH)

    @pl.when(core == 0)
    def _():
        pl.semaphore_wait(go_z, 1)

    def along_row(i):
        return pltpu.make_async_remote_copy(
            src_ref=blocks.at[z], dst_ref=blocks.at[z], send_sem=sz.at[i], recv_sem=rz.at[z],
            device_id=(y * nz + lax.rem(z + i, nz), tp), device_id_type=MESH,
        )

    for i in (4, 3, 5, 2, 6, 1, 7):
        along_row(i).start()

    expand = jnp.where(
        (iota((128, 96), 1) == lax.div(iota((128, 96), 0), SLAB) * 12 + lax.rem(iota((128, 96), 0), SLAB))
        & (lax.rem(iota((128, 96), 0), SLAB) < 12),
        1.0, 0.0,
    ).astype(BF)
    ones = jnp.ones((128, 256), BF)
    in_slab = lax.rem(iota((128, 128), 0), SLAB)

    def back_to(b, i):
        to_y = lax.rem(y + i, ny)
        return pltpu.make_async_remote_copy(
            src_ref=msgs.at[b, to_y], dst_ref=back.at[z, y], send_sem=sr.at[b, i], recv_sem=rr.at[z, y],
            device_id=(to_y * nz + b, tp), device_id_type=MESH,
        )

    def one_block(b, carry):
        @pl.when(b != z)
        def _():
            pltpu.make_async_remote_copy(
                src_ref=blocks.at[b], dst_ref=blocks.at[b], send_sem=sz.at[0], recv_sem=rz.at[b],
                device_id=(kv, tp), device_id_type=MESH,
            ).wait_recv()

        q = blocks[b]
        total = jnp.zeros((96, 128), F32)
        out = jnp.zeros((96, HD), F32)
        for c in range(8):
            at = pl.ds(c * CHUNK, CHUNK)
            e = jnp.exp2(jnp.tanh(nt(q, kv_v[0, at]) * sc_v[0, :, at]) * (50.0 * LOG2E))
            total += e[:, :128] + e[:, 128:]
            out += mm((e * sc_v[1, :, at]).astype(BF), kv_v[1, at])
        high, low = split(total)
        wide = mm(expand, jnp.concatenate([out.astype(BF), high, low], axis=1))
        totals = nt(ones, wide[:, 128:].astype(BF))
        high, low = split(totals)
        msg = jnp.where(in_slab == 12, high.astype(F32), jnp.where(in_slab == 13, low.astype(F32), wide[:, :HD]))
        msgs[b] = msg.astype(BF).reshape(NPRE, SLAB, HD)
        for i in (4, 3, 5, 2, 6, 1, 7):
            back_to(b, i).start()

        @pl.when(b != z)
        def _():
            back_to(b, 0).start()

        @pl.when(b == z)
        def _():
            back[z, y] = msgs[z, y]

        return carry

    lax.fori_loop(0, nz, one_block, 0)

    def wait_back(j, carry):
        a, b = lax.div(j, ny), lax.rem(j, ny)

        @pl.when((a != z) | (b != y))
        def _():
            pltpu.make_async_remote_copy(
                src_ref=back.at[a, b], dst_ref=back.at[a, b], send_sem=sr.at[0, 0], recv_sem=rr.at[a, b],
                device_id=(kv, tp), device_id_type=MESH,
            ).wait_recv()

        return carry

    lax.fori_loop(0, nz * ny, wait_back, 0)
    summed = back[0].astype(F32)
    for a in range(1, 8):
        summed += back[a].astype(F32)
    high, low = split(summed.reshape(128, HD))
    held = jnp.concatenate([high, low], axis=0)
    lane = iota((16, 256), 1) & 127
    first = (ids * SLAB).astype(jnp.int32)
    picks = [jnp.where(lane == place + h * SLOTS, 1.0, 0.0) for h in range(2)]
    pick_total = jnp.where((lane == first + 12) | (lane == first + 13), 1.0, 0.0)
    found = mm(jnp.concatenate([picks[0], picks[1], pick_total, pick_total], axis=0).astype(BF), held)
    total_rows = found[32:]
    rank_lane = y * SLAB + rank.astype(jnp.int32)
    total = jnp.concatenate(
        [
            jnp.sum(jnp.where(lane16 == rank_lane + h * SLOTS, total_rows[:16], 0.0), axis=1, keepdims=True)
            for h in range(2)
        ],
        axis=0,
    )
    att = ((found[:32] + suf_out) / (total + suf_total)).astype(BF)
    att = jnp.concatenate([att[:16], att[16:]], axis=1)

    got_w.wait()

    def to_group(i, c):
        return pltpu.make_async_remote_copy(
            src_ref=part.at[i, c], dst_ref=parts.at[tp], send_sem=sx.at[i, c], recv_sem=rx.at[tp],
            device_id=(kv, lax.rem(x + i, nx) * 2 + c), device_id_type=MESH,
        )

    for i in (2, 1, 3, 0):
        at = pl.multiple_of(lax.rem(x + i, nx) * 1152, 128)
        got = mm(att, w_v[:, pl.ds(at, 1152)])
        part[i, 0] = got[:, :640].astype(BF)
        part[i, 1] = got[:, 512:].astype(BF)
        if i:
            to_group(i, 0).start()
            to_group(i, 1).start()
        else:
            own = jnp.where(core == 0, got[:, :640], got[:, 512:])
            pltpu.make_async_remote_copy(
                src_ref=part.at[0, 1 - core], dst_ref=parts.at[tp], send_sem=sx.at[0, 0], recv_sem=rx.at[tp],
                device_id=(kv, x * 2 + (1 - core)), device_id_type=MESH,
            ).start()
    got_res.wait()
    got_gain.wait()
    for i in range(1, 8):
        t = lax.rem(tp + i, 8)
        pltpu.make_async_remote_copy(
            src_ref=parts.at[t], dst_ref=parts.at[t], send_sem=sx.at[0, 0], recv_sem=rx.at[t],
            device_id=(kv, tp), device_id_type=MESH,
        ).wait_recv()
        own += parts[t].astype(F32)
    own = jnp.where(core == 0, own[:, :576], own[:, 64:])
    square[...] = jnp.broadcast_to(jnp.sum(own * own, axis=1, keepdims=True), (16, 128))

    def to_square(i):
        return pltpu.make_async_remote_copy(
            src_ref=square, dst_ref=squares.at[tp], send_sem=ss.at[i], recv_sem=rs.at[tp],
            device_id=(kv, lax.rem(tp + i, 8)), device_id_type=MESH,
        )

    for i in (4, 5, 3, 2, 6, 1, 7):
        to_square(i).start()
    resid = res_v[...].astype(F32)
    gained = own * gain_v[...].reshape(1, 576)
    sq = square[...]
    for i in range(1, 8):
        t = lax.rem(tp + i, 8)
        pltpu.make_async_remote_copy(
            src_ref=square, dst_ref=squares.at[t], send_sem=ss.at[0], recv_sem=rs.at[t],
            device_id=(kv, tp), device_id_type=MESH,
        ).wait_recv()
        sq += squares[t]
    scale = lax.rsqrt(sq[:, :1] / 4608.0 + 1e-06)
    o_ref[...] = (resid + gained * scale).astype(BF)

    for i in range(1, 8):
        to_holder(i).wait_send()
        along_row(i).wait_send()
        to_square(i).wait_send()
    for i in range(1, nx):
        to_group(i, 0).wait_send()
        to_group(i, 1).wait_send()
    to_group(0, 0).wait_send()

    def wait_sent(j, carry):
        b, i = lax.div(j, ny), lax.rem(j, ny)

        @pl.when((b != z) | (i != 0))
        def _():
            back_to(b, i).wait_send()

        return carry

    lax.fori_loop(0, nz * ny, wait_sent, 0)


def local(q, ids, kv, scales, suf, lens, w, res, gain):
    nz = ny = 8
    nx = lax.axis_size("tp") // 2
    hbm = pl.BlockSpec(memory_space=pl.ANY)
    vmem = pl.BlockSpec(memory_space=pltpu.VMEM)
    dma = pltpu.SemaphoreType.DMA

    def body(*refs):
        kernel(nz, ny, nx, *refs)

    return pl.pallas_call(
        body,
        out_shape=jax.ShapeDtypeStruct(res.shape, BF),
        in_specs=[hbm, vmem, hbm, hbm, hbm, vmem, hbm, hbm, hbm],
        out_specs=vmem,
        scratch_shapes=[
            pltpu.VMEM((16, 256), BF),
            pltpu.VMEM((2, 2048, 128), BF),
            pltpu.VMEM((2, 1, 2048), F32),
            pltpu.VMEM((2, 16, 128, 128), BF),
            pltpu.VMEM((256, 4608), BF),
            pltpu.VMEM((16, 576), BF),
            pltpu.VMEM((576,), F32),
            pltpu.VMEM((8, 16, 128), BF),
            pltpu.VMEM((8, 16, 128), BF),
            pltpu.VMEM((8, 96, 128), BF),
            pltpu.VMEM((8, 8, 16, 128), BF),
            pltpu.VMEM((8, 8, 16, 128), BF),
            pltpu.VMEM((4, 2, 16, 640), BF),
            pltpu.VMEM((8, 16, 640), BF),
            pltpu.VMEM((16, 128), F32),
            pltpu.VMEM((8, 16, 128), F32),
            pltpu.VMEM((16, 576), BF),
            dma((7,)),
            pltpu.SemaphoreType.REGULAR,
            pltpu.SemaphoreType.REGULAR,
            dma((8,)), dma((8,)), dma((8,)), dma((8,)),
            dma((8, 8)), dma((8, 8)),
            dma((4, 2)), dma((8,)), dma((8,)), dma((8,)),
        ],
        compiler_params=pltpu.CompilerParams(
            collective_id=0, has_side_effects=True, vmem_limit_bytes=62 * 2**20
        ),
        cost_estimate=pl.CostEstimate(flops=10**9, bytes_accessed=5 * 10**6, transcendentals=3 * 10**6),
        name="attend",
    )(q, ids.reshape(1, 16), kv, scales, suf, lens.reshape(1, 16), w, res, gain)


def solution(mesh):
    placed = (
        P("kv", "tp"), P("kv", None), P(None, "kv", "tp"), P(None, "tp", "kv"), P(None, "kv", None, "tp"),
        P("kv"), P("tp", None), P("kv", "tp"), P("tp"),
    )
    return jax.shard_map(local, mesh=mesh, in_specs=placed, out_specs=P("kv", "tp"), check_vma=False)
```

```python
import jax
import jax.numpy as jnp
from jax import lax
from jax.experimental import pallas as pl
from jax.experimental.pallas import tpu as pltpu
from jax.sharding import PartitionSpec as P

HD = 128
NPRE = 8
SLOTS = 6
SLAB = 16
MESH = pl.DeviceIdType.MESH
BF = jnp.bfloat16
F32 = jnp.float32
LOG2E = 1.4426950408889634
SCORE = 144.0 ** (-0.5)
CHUNK = 256


def iota(shape, dim):
    return lax.broadcasted_iota(jnp.int32, shape, dim)


def nt(a, b):
    return lax.dot_general(a, b, (((1,), (1,)), ((), ())), preferred_element_type=F32)


def mm(a, b):
    return jnp.dot(a, b, preferred_element_type=F32)


def split(a):
    high = a.astype(BF)
    return high, (a - high.astype(F32)).astype(BF)


def kernel(
    nz, ny, nx,
    q_ref, ids_ref, kv_ref, scales_ref, suf_ref, len_ref, w_ref, res_ref, gain_ref,
    o_ref,
    q_v, ids_v, len_v, kv_v, sc_v, suf_v, w_v, res_v, gain_v,
    slots, gathered, blocks, msgs, back, part, parts, square, squares, out_v,
    local_sem, go_y, go_z, sy, ry, sz, rz, sr, rr, sx, rx, ss, rs,
):
    kv, tp = lax.axis_index("kv"), lax.axis_index("tp")
    y, z = lax.div(kv, nz), lax.rem(kv, nz)
    x, core = lax.div(tp, 2), lax.rem(tp, 2)

    barrier = pltpu.get_barrier_semaphore()

    def here(to_kv, to_tp):
        pl.semaphore_signal(barrier, inc=1, device_id=(to_kv, to_tp), device_id_type=MESH)

    here(kv, x * 2 + (1 - core))
    for i in (4, 3, 5, 2, 6, 1, 7):
        here(lax.rem(y + i, ny) * nz + z, x * 2)
    for i in (4, 3, 5, 2, 6, 1, 7):
        here(y * nz + lax.rem(z + i, nz), x * 2 + 1)
    for i in (2, 1, 3):
        here(kv, lax.rem(x + i, nx) * 2 + 1)

    def fetch(i, src, dst):
        c = pltpu.make_async_copy(src, dst, local_sem.at[i])
        c.start()
        return c

    got_q = fetch(0, q_ref, q_v)
    got_ids = fetch(7, ids_ref, ids_v)
    got_len = fetch(8, len_ref, len_v)
    got_kv = fetch(1, kv_ref, kv_v)
    got_sc = fetch(2, scales_ref, sc_v)
    got_suf = fetch(3, suf_ref, suf_v)
    got_w = fetch(4, w_ref, w_v)
    got_res = fetch(5, res_ref, res_v)
    got_gain = fetch(6, gain_ref, gain_v)

    row16, lane16 = iota((16, 128), 0), iota((16, 128), 1)
    got_ids.wait()
    ids_row = ids_v[...].astype(F32)
    square16 = iota((16, 16), 0), iota((16, 16), 1)
    ids = jnp.sum(jnp.where(square16[0] == square16[1], ids_row, 0.0), axis=1, keepdims=True)
    same = jnp.where(ids == ids_row, 1.0, 0.0)
    rank = jnp.sum(jnp.where(square16[1] < square16[0], same, 0.0), axis=1, keepdims=True)
    rank_row = jnp.sum(jnp.where(square16[0] < square16[1], same, 0.0), axis=0, keepdims=True)
    place = (ids * SLAB + rank).astype(jnp.int32)
    place_row = (ids_row * SLAB + rank_row).astype(jnp.int32)

    got_q.wait()
    row128 = iota((128, 16), 0)
    picks = [jnp.where(row128 == place_row + h * SLOTS, 1.0, 0.0).astype(BF) for h in range(2)]
    slotted = mm(picks[0], q_v[:, :HD]) + mm(picks[1], q_v[:, HD:])
    slots[...] = slotted.astype(BF).reshape(NPRE, SLAB, HD)

    @pl.when(core == 0)
    def _():
        pl.semaphore_wait(barrier, 2 * (ny - 1) + 1)
        pl.semaphore_signal(go_y, inc=1, device_id=(kv, tp + 1), device_id_type=MESH)

    @pl.when(core == 1)
    def _():
        pl.semaphore_wait(go_y, 1)

    def to_holder(i):
        p = lax.rem(y + i, ny)
        return pltpu.make_async_remote_copy(
            src_ref=slots.at[p], dst_ref=gathered.at[y], send_sem=sy.at[i], recv_sem=ry,
            device_id=(p * nz + z, tp), device_id_type=MESH,
        )

    for i in (4, 3, 5, 2, 6, 1, 7):
        to_holder(i).start()
    pltpu.make_async_copy(slots.at[y], gathered.at[y], ry).start()

    got_suf.wait()
    got_len.wait()
    eye = jnp.where(iota((32, 16), 1) == lax.rem(iota((32, 16), 0), 16), 1.0, 0.0)
    lens = jnp.sum(eye * len_v[...].astype(F32), axis=1, keepdims=True).astype(jnp.int32)
    own_q = jnp.concatenate([q_v[:, :HD], q_v[:, HD:]], axis=0)
    own_request = lax.rem(iota((32, CHUNK), 0), 16)
    suf_out = jnp.zeros((32, HD), F32)
    suf_total = jnp.zeros((32, 128), F32)
    for c in range(8):
        k = suf_v[0, 2 * c : 2 * c + 2].reshape(CHUNK, HD)
        v = suf_v[1, 2 * c : 2 * c + 2].reshape(CHUNK, HD)
        e = jnp.exp2(jnp.tanh(nt(own_q, k) * (SCORE / 50.0)) * (50.0 * LOG2E))
        at = iota((32, CHUNK), 1)
        live = (lax.div(at, 128) + 2 * c == own_request) & (lax.rem(at, 128) < lens)
        e = jnp.where(live, e, 0.0)
        suf_total += e[:, :128] + e[:, 128:]
        suf_out += mm(e.astype(BF), v)
    suf_total = jnp.sum(suf_total, axis=1, keepdims=True)

    got_kv.wait()
    got_sc.wait()
    sc_v[0] = sc_v[0] * (SCORE / 50.0)

    pltpu.make_async_copy(gathered, gathered, ry).wait()
    compact = jnp.where(
        iota((96, 128), 1) == lax.div(iota((96, 128), 0), 12) * SLAB + lax.rem(iota((96, 128), 0), 12), 1.0, 0.0
    ).astype(BF)
    blocks[z] = mm(compact, gathered[...].reshape(128, HD)).astype(BF)

    @pl.when(core == 1)
    def _():
        pl.semaphore_wait(barrier, 2 * (nz - 1) + 1 + 2 * (nx - 1))
        pl.semaphore_signal(go_z, inc=1, device_id=(kv, tp - 1), device_id_type=MESH)

    @pl.when(core == 0)
    def _():
        pl.semaphore_wait(go_z, 1)

    def along_row(i):
        return pltpu.make_async_remote_copy(
            src_ref=blocks.at[z], dst_ref=blocks.at[z], send_sem=sz.at[i], recv_sem=rz.at[z],
            device_id=(y * nz + lax.rem(z + i, nz), tp), device_id_type=MESH,
        )

    for i in (4, 3, 5, 2, 6, 1, 7):
        along_row(i).start()

    expand = jnp.where(
        (iota((128, 96), 1) == lax.div(iota((128, 96), 0), SLAB) * 12 + lax.rem(iota((128, 96), 0), SLAB))
        & (lax.rem(iota((128, 96), 0), SLAB) < 12),
        1.0, 0.0,
    ).astype(BF)
    ones = jnp.ones((128, 256), BF)
    in_slab = lax.rem(iota((128, 128), 0), SLAB)

    def back_to(b, i):
        to_y = lax.rem(y + i, ny)
        return pltpu.make_async_remote_copy(
            src_ref=msgs.at[b * ny + to_y], dst_ref=back.at[z, y], send_sem=sr, recv_sem=rr,
            device_id=(to_y * nz + b, tp), device_id_type=MESH,
        )

    def two_blocks(step, carry):
        for j in range(2):
            b = step * 2 + j

            @pl.when(b != z)
            def _():
                pltpu.make_async_remote_copy(
                    src_ref=blocks.at[b], dst_ref=blocks.at[b], send_sem=sz.at[0], recv_sem=rz.at[b],
                    device_id=(kv, tp), device_id_type=MESH,
                ).wait_recv()

        q = blocks[pl.ds(step * 2, 2)].reshape(192, HD)
        total = jnp.zeros((192, 128), F32)
        out = jnp.zeros((192, HD), F32)
        for n in range(2):
            at = pl.ds(n * 1024, 1024)
            e = jnp.exp2(jnp.tanh(nt(q, kv_v[0, at]) * sc_v[0, :, at]) * (50.0 * LOG2E))
            for c in range(8):
                total += e[:, c * 128 : (c + 1) * 128]
            out += mm((e * sc_v[1, :, at]).astype(BF), kv_v[1, at])
        high, low = split(total)
        rows = jnp.concatenate([out.astype(BF), high, low], axis=1)
        for j in range(2):
            b = step * 2 + j
            wide = mm(expand, rows[j * 96 : j * 96 + 96])
            totals = nt(ones, wide[:, 128:].astype(BF))
            high, low = split(totals)
            msg = jnp.where(in_slab == 12, high.astype(F32), jnp.where(in_slab == 13, low.astype(F32), wide[:, :HD]))
            msgs[pl.ds(b * ny, ny)] = msg.astype(BF).reshape(NPRE, SLAB, HD)
        for j in range(2):
            b = step * 2 + j
            for i in (4, 3, 5, 2, 6, 1, 7):
                back_to(b, i).start()

            @pl.when(b != z)
            def _():
                back_to(b, 0).start()

            @pl.when(b == z)
            def _():
                pltpu.make_async_copy(msgs.at[z * ny + y], back.at[z, y], rr).start()

        return carry

    lax.fori_loop(0, nz // 2, two_blocks, 0)

    pltpu.make_async_copy(back, back, rr).wait()
    summed = back[0].astype(F32)
    for a in range(1, 8):
        summed += back[a].astype(F32)
    high, low = split(summed.reshape(128, HD))
    held = jnp.concatenate([high, low], axis=0)
    lane = iota((16, 256), 1) & 127
    first = (ids * SLAB).astype(jnp.int32)
    picks = [jnp.where(lane == place + h * SLOTS, 1.0, 0.0) for h in range(2)]
    pick_total = jnp.where((lane == first + 12) | (lane == first + 13), 1.0, 0.0)
    found = mm(jnp.concatenate([picks[0], picks[1], pick_total, pick_total], axis=0).astype(BF), held)
    total_rows = found[32:]
    rank_lane = y * SLAB + rank.astype(jnp.int32)
    total = jnp.concatenate(
        [
            jnp.sum(jnp.where(lane16 == rank_lane + h * SLOTS, total_rows[:16], 0.0), axis=1, keepdims=True)
            for h in range(2)
        ],
        axis=0,
    )
    att = ((found[:32] + suf_out) / (total + suf_total)).astype(BF)
    att = jnp.concatenate([att[:16], att[16:]], axis=1)

    got_w.wait()

    def to_group(i, c):
        return pltpu.make_async_remote_copy(
            src_ref=part.at[i, c], dst_ref=parts.at[tp], send_sem=sx.at[i, c], recv_sem=rx.at[tp],
            device_id=(kv, lax.rem(x + i, nx) * 2 + c), device_id_type=MESH,
        )

    for i in (2, 1, 3, 0):
        at = pl.multiple_of(lax.rem(x + i, nx) * 1152, 128)
        got = mm(att, w_v[:, pl.ds(at, 1152)])
        part[i, 0] = got[:, :640].astype(BF)
        part[i, 1] = got[:, 512:].astype(BF)
        if i:
            to_group(i, 0).start()
            to_group(i, 1).start()
        else:
            own = jnp.where(core == 0, got[:, :640], got[:, 512:])
            pltpu.make_async_remote_copy(
                src_ref=part.at[0, 1 - core], dst_ref=parts.at[tp], send_sem=sx.at[0, 0], recv_sem=rx.at[tp],
                device_id=(kv, x * 2 + (1 - core)), device_id_type=MESH,
            ).start()
    got_res.wait()
    got_gain.wait()
    for i in range(1, 8):
        t = lax.rem(tp + i, 8)
        pltpu.make_async_remote_copy(
            src_ref=parts.at[t], dst_ref=parts.at[t], send_sem=sx.at[0, 0], recv_sem=rx.at[t],
            device_id=(kv, tp), device_id_type=MESH,
        ).wait_recv()
        own += parts[t].astype(F32)
    own = jnp.where(core == 0, own[:, :576], own[:, 64:])
    square[...] = jnp.sum(
        jnp.where(row16 == lane16, jnp.sum(own * own, axis=1, keepdims=True), 0.0), axis=0, keepdims=True
    )

    def to_square(i):
        return pltpu.make_async_remote_copy(
            src_ref=square, dst_ref=squares.at[tp], send_sem=ss.at[i], recv_sem=rs.at[tp],
            device_id=(kv, lax.rem(tp + i, 8)), device_id_type=MESH,
        )

    for i in (4, 5, 3, 2, 6, 1, 7):
        to_square(i).start()
    resid = res_v[...].astype(F32)
    gained = own * gain_v[...].reshape(1, 576)
    sq = square[...]
    for i in range(1, 8):
        t = lax.rem(tp + i, 8)
        pltpu.make_async_remote_copy(
            src_ref=square, dst_ref=squares.at[t], send_sem=ss.at[0], recv_sem=rs.at[t],
            device_id=(kv, tp), device_id_type=MESH,
        ).wait_recv()
        sq += squares[t]
    sq = jnp.sum(jnp.where(row16 == lane16, sq, 0.0), axis=1, keepdims=True)
    scale = lax.rsqrt(sq / 4608.0 + 1e-06)
    o_ref[...] = (resid + gained * scale).astype(BF)

    for i in range(1, 8):
        to_holder(i).wait_send()
        along_row(i).wait_send()
        to_square(i).wait_send()
    for i in range(1, nx):
        to_group(i, 0).wait_send()
        to_group(i, 1).wait_send()
    to_group(0, 0).wait_send()

    sent = msgs.at[pl.ds(0, nz * ny - 1)]
    pltpu.make_async_copy(sent, sent, sr).wait()


def local(q, ids, kv, scales, suf, lens, w, res, gain):
    nz = ny = 8
    nx = lax.axis_size("tp") // 2
    hbm = pl.BlockSpec(memory_space=pl.ANY)
    vmem = pl.BlockSpec(memory_space=pltpu.VMEM)
    dma = pltpu.SemaphoreType.DMA

    def body(*refs):
        kernel(nz, ny, nx, *refs)

    return pl.pallas_call(
        body,
        out_shape=jax.ShapeDtypeStruct(res.shape, BF),
        in_specs=[hbm] * 9,
        out_specs=vmem,
        scratch_shapes=[
            pltpu.VMEM((16, 256), BF),
            pltpu.VMEM((1, 16), jnp.int32),
            pltpu.VMEM((1, 16), jnp.int32),
            pltpu.VMEM((2, 2048, 128), BF),
            pltpu.VMEM((2, 1, 2048), F32),
            pltpu.VMEM((2, 16, 128, 128), BF),
            pltpu.VMEM((256, 4608), BF),
            pltpu.VMEM((16, 576), BF),
            pltpu.VMEM((576,), F32),
            pltpu.VMEM((8, 16, 128), BF),
            pltpu.VMEM((8, 16, 128), BF),
            pltpu.VMEM((8, 96, 128), BF),
            pltpu.VMEM((64, 16, 128), BF),
            pltpu.VMEM((8, 8, 16, 128), BF),
            pltpu.VMEM((4, 2, 16, 640), BF),
            pltpu.VMEM((8, 16, 640), BF),
            pltpu.VMEM((1, 128), F32),
            pltpu.VMEM((8, 1, 128), F32),
            pltpu.VMEM((16, 576), BF),
            dma((9,)),
            pltpu.SemaphoreType.REGULAR,
            pltpu.SemaphoreType.REGULAR,
            dma((8,)), dma, dma((8,)), dma((8,)),
            dma, dma,
            dma((4, 2)), dma((8,)), dma((8,)), dma((8,)),
        ],
        compiler_params=pltpu.CompilerParams(
            collective_id=0, has_side_effects=True, vmem_limit_bytes=62 * 2**20
        ),
        cost_estimate=pl.CostEstimate(flops=10**9, bytes_accessed=5 * 10**6, transcendentals=3 * 10**6),
        name="attend",
    )(q, ids.reshape(1, 16), kv, scales, suf, lens.reshape(1, 16), w, res, gain)


def solution(mesh):
    placed = (
        P("kv", "tp"), P("kv", None), P(None, "kv", "tp"), P(None, "tp", "kv"), P(None, "kv", None, "tp"),
        P("kv"), P("tp", None), P("kv", "tp"), P("tp"),
    )
    return jax.shard_map(local, mesh=mesh, in_specs=placed, out_specs=P("kv", "tp"), check_vma=False)
```

```python
import jax
import jax.numpy as jnp
from jax import lax
from jax.experimental import pallas as pl
from jax.experimental.pallas import tpu as pltpu
from jax.sharding import PartitionSpec as P

HD = 128
NPRE = 8
SLOTS = 6
SLAB = 16
MESH = pl.DeviceIdType.MESH
BF = jnp.bfloat16
F32 = jnp.float32
LOG2E = 1.4426950408889634
SCORE = 144.0 ** (-0.5)
CHUNK = 256


def iota(shape, dim):
    return lax.broadcasted_iota(jnp.int32, shape, dim)


def nt(a, b):
    return lax.dot_general(a, b, (((1,), (1,)), ((), ())), preferred_element_type=F32)


def mm(a, b):
    return jnp.dot(a, b, preferred_element_type=F32)


def split(a):
    high = a.astype(BF)
    return high, (a - high.astype(F32)).astype(BF)


def kernel(
    nz, ny, nx,
    q_ref, ids_ref, kv_ref, scales_ref, suf_ref, len_ref, w_ref, res_ref, gain_ref,
    o_ref,
    q_v, ids_v, len_v, kv_v, sc_v, suf_v, w_v, res_v, gain_v,
    slots, gathered, blocks, msgs, back, part, parts, square, squares, out_v,
    local_sem, go_y, go_z, sy, ry, sz, rz, sr, rr, sx, rx, ss, rs,
):
    kv, tp = lax.axis_index("kv"), lax.axis_index("tp")
    y, z = lax.div(kv, nz), lax.rem(kv, nz)
    x, core = lax.div(tp, 2), lax.rem(tp, 2)

    barrier = pltpu.get_barrier_semaphore()

    def here(to_kv, to_tp):
        pl.semaphore_signal(barrier, inc=1, device_id=(to_kv, to_tp), device_id_type=MESH)

    late = nz // 2
    here(kv, x * 2 + (1 - core))
    for i in (4, 3, 5, 2, 6, 1, 7):
        here(lax.rem(y + i, ny) * nz + z, x * 2)
    for i in (4, 3, 5, 2, 6, 1, 7):
        here(y * nz + lax.rem(z + i, nz), x * 2 + jnp.where(z < late, 0, 1))
    for i in (2, 1, 3):
        here(kv, lax.rem(x + i, nx) * 2 + 1)

    def fetch(i, src, dst):
        c = pltpu.make_async_copy(src, dst, local_sem.at[i])
        c.start()
        return c

    got_q = fetch(0, q_ref, q_v)
    got_ids = fetch(7, ids_ref, ids_v)
    got_len = fetch(8, len_ref, len_v)
    got_kv = fetch(1, kv_ref, kv_v)
    got_sc = fetch(2, scales_ref, sc_v)
    got_suf = fetch(3, suf_ref, suf_v)
    got_w = fetch(4, w_ref, w_v)
    got_res = fetch(5, res_ref, res_v)
    got_gain = fetch(6, gain_ref, gain_v)

    row16, lane16 = iota((16, 128), 0), iota((16, 128), 1)
    got_ids.wait()
    ids_row = ids_v[...].astype(F32)
    square16 = iota((16, 16), 0), iota((16, 16), 1)
    ids = jnp.sum(jnp.where(square16[0] == square16[1], ids_row, 0.0), axis=1, keepdims=True)
    same = jnp.where(ids == ids_row, 1.0, 0.0)
    rank = jnp.sum(jnp.where(square16[1] < square16[0], same, 0.0), axis=1, keepdims=True)
    rank_row = jnp.sum(jnp.where(square16[0] < square16[1], same, 0.0), axis=0, keepdims=True)
    place = (ids * SLAB + rank).astype(jnp.int32)
    place_row = (ids_row * SLAB + rank_row).astype(jnp.int32)

    got_q.wait()
    row128 = iota((128, 16), 0)
    picks = [jnp.where(row128 == place_row + h * SLOTS, 1.0, 0.0).astype(BF) for h in range(2)]
    slotted = mm(picks[0], q_v[:, :HD]) + mm(picks[1], q_v[:, HD:])
    slots[...] = slotted.astype(BF).reshape(NPRE, SLAB, HD)

    @pl.when(core == 0)
    def _():
        pl.semaphore_wait(barrier, 1 + 2 * (ny - 1) + 2 * jnp.where(z < late, late - 1, late))
        pl.semaphore_signal(go_y, inc=1, device_id=(kv, tp + 1), device_id_type=MESH)

    @pl.when(core == 1)
    def _():
        pl.semaphore_wait(go_y, 1)

    def to_holder(i):
        p = lax.rem(y + i, ny)
        return pltpu.make_async_remote_copy(
            src_ref=slots.at[p], dst_ref=gathered.at[y], send_sem=sy.at[i], recv_sem=ry,
            device_id=(p * nz + z, tp), device_id_type=MESH,
        )

    for i in (4, 3, 5, 2, 6, 1, 7):
        to_holder(i).start()
    pltpu.make_async_copy(slots.at[y], gathered.at[y], ry).start()

    got_suf.wait()
    got_len.wait()
    eye = jnp.where(iota((32, 16), 1) == lax.rem(iota((32, 16), 0), 16), 1.0, 0.0)
    lens = jnp.sum(eye * len_v[...].astype(F32), axis=1, keepdims=True).astype(jnp.int32)
    own_q = jnp.concatenate([q_v[:, :HD], q_v[:, HD:]], axis=0)
    own_request = lax.rem(iota((32, CHUNK), 0), 16)
    suf_out = jnp.zeros((32, HD), F32)
    suf_total = jnp.zeros((32, 128), F32)
    for c in range(8):
        k = suf_v[0, 2 * c : 2 * c + 2].reshape(CHUNK, HD)
        v = suf_v[1, 2 * c : 2 * c + 2].reshape(CHUNK, HD)
        e = jnp.exp2(jnp.tanh(nt(own_q, k) * (SCORE / 50.0)) * (50.0 * LOG2E))
        at = iota((32, CHUNK), 1)
        live = (lax.div(at, 128) + 2 * c == own_request) & (lax.rem(at, 128) < lens)
        e = jnp.where(live, e, 0.0)
        suf_total += e[:, :128] + e[:, 128:]
        suf_out += mm(e.astype(BF), v)
    suf_total = jnp.sum(suf_total, axis=1, keepdims=True)

    got_kv.wait()
    got_sc.wait()
    sc_v[0] = sc_v[0] * (SCORE / 50.0)

    pltpu.make_async_copy(gathered, gathered, ry).wait()
    compact = jnp.where(
        iota((96, 128), 1) == lax.div(iota((96, 128), 0), 12) * SLAB + lax.rem(iota((96, 128), 0), 12), 1.0, 0.0
    ).astype(BF)
    blocks[z] = mm(compact, gathered[...].reshape(128, HD)).astype(BF)

    def along_row(i):
        return pltpu.make_async_remote_copy(
            src_ref=blocks.at[z], dst_ref=blocks.at[z], send_sem=sz.at[i], recv_sem=rz.at[z],
            device_id=(y * nz + lax.rem(z + i, nz), tp), device_id_type=MESH,
        )

    def to_half(half):
        for i in (4, 3, 5, 2, 6, 1, 7):

            @pl.when(lax.div(lax.rem(z + i, nz), late) == half)
            def _():
                along_row(i).start()

    to_half(0)

    @pl.when(core == 1)
    def _():
        pl.semaphore_wait(barrier, 1 + 2 * (nx - 1) + 2 * jnp.where(z < late, late, late - 1))
        pl.semaphore_signal(go_z, inc=1, device_id=(kv, tp - 1), device_id_type=MESH)

    @pl.when(core == 0)
    def _():
        pl.semaphore_wait(go_z, 1)

    to_half(1)


    expand = jnp.where(
        (iota((128, 96), 1) == lax.div(iota((128, 96), 0), SLAB) * 12 + lax.rem(iota((128, 96), 0), SLAB))
        & (lax.rem(iota((128, 96), 0), SLAB) < 12),
        1.0, 0.0,
    ).astype(BF)
    ones = jnp.ones((128, 256), BF)
    in_slab = lax.rem(iota((128, 128), 0), SLAB)

    def back_to(b, i):
        to_y = lax.rem(y + i, ny)
        return pltpu.make_async_remote_copy(
            src_ref=msgs.at[b * ny + to_y], dst_ref=back.at[z, y], send_sem=sr, recv_sem=rr,
            device_id=(to_y * nz + b, tp), device_id_type=MESH,
        )

    def one_block(b, carry):
        @pl.when(b != z)
        def _():
            pltpu.make_async_remote_copy(
                src_ref=blocks.at[b], dst_ref=blocks.at[b], send_sem=sz.at[0], recv_sem=rz.at[b],
                device_id=(kv, tp), device_id_type=MESH,
            ).wait_recv()

        q = blocks[b]
        total = jnp.zeros((96, 128), F32)
        out = jnp.zeros((96, HD), F32)
        e = jnp.exp2(jnp.tanh(nt(q, kv_v[0]) * sc_v[0]) * (50.0 * LOG2E))
        for c in range(16):
            total += e[:, c * 128 : (c + 1) * 128]
        out += mm((e * sc_v[1]).astype(BF), kv_v[1])
        high, low = split(total)
        wide = mm(expand, jnp.concatenate([out.astype(BF), high, low], axis=1))
        totals = nt(ones, wide[:, 128:].astype(BF))
        high, low = split(totals)
        msg = jnp.where(in_slab == 12, high.astype(F32), jnp.where(in_slab == 13, low.astype(F32), wide[:, :HD]))
        msgs[pl.ds(b * ny, ny)] = msg.astype(BF).reshape(NPRE, SLAB, HD)
        for i in (4, 3, 5, 2, 6, 1, 7):
            back_to(b, i).start()

        @pl.when(b != z)
        def _():
            back_to(b, 0).start()

        @pl.when(b == z)
        def _():
            pltpu.make_async_copy(msgs.at[z * ny + y], back.at[z, y], rr).start()

        return carry

    lax.fori_loop(0, nz, one_block, 0)

    pltpu.make_async_copy(back, back, rr).wait()
    summed = back[0].astype(F32)
    for a in range(1, 8):
        summed += back[a].astype(F32)
    high, low = split(summed.reshape(128, HD))
    held = jnp.concatenate([high, low], axis=0)
    lane = iota((16, 256), 1) & 127
    first = (ids * SLAB).astype(jnp.int32)
    picks = [jnp.where(lane == place + h * SLOTS, 1.0, 0.0) for h in range(2)]
    pick_total = jnp.where((lane == first + 12) | (lane == first + 13), 1.0, 0.0)
    found = mm(jnp.concatenate([picks[0], picks[1], pick_total, pick_total], axis=0).astype(BF), held)
    total_rows = found[32:]
    rank_lane = y * SLAB + rank.astype(jnp.int32)
    total = jnp.concatenate(
        [
            jnp.sum(jnp.where(lane16 == rank_lane + h * SLOTS, total_rows[:16], 0.0), axis=1, keepdims=True)
            for h in range(2)
        ],
        axis=0,
    )
    att = ((found[:32] + suf_out) / (total + suf_total)).astype(BF)
    att = jnp.concatenate([att[:16], att[16:]], axis=1)

    got_w.wait()

    def to_group(i, c):
        return pltpu.make_async_remote_copy(
            src_ref=part.at[i, c], dst_ref=parts.at[tp], send_sem=sx.at[i, c], recv_sem=rx.at[tp],
            device_id=(kv, lax.rem(x + i, nx) * 2 + c), device_id_type=MESH,
        )

    for i in (2, 1, 3, 0):
        at = pl.multiple_of(lax.rem(x + i, nx) * 1152, 128)
        got = mm(att, w_v[:, pl.ds(at, 1152)])
        part[i, 0] = got[:, :640].astype(BF)
        part[i, 1] = got[:, 512:].astype(BF)
        if i:
            to_group(i, 0).start()
            to_group(i, 1).start()
        else:
            own = jnp.where(core == 0, got[:, :640], got[:, 512:])
            pltpu.make_async_remote_copy(
                src_ref=part.at[0, 1 - core], dst_ref=parts.at[tp], send_sem=sx.at[0, 0], recv_sem=rx.at[tp],
                device_id=(kv, x * 2 + (1 - core)), device_id_type=MESH,
            ).start()
    got_res.wait()
    got_gain.wait()
    for i in range(1, 8):
        t = lax.rem(tp + i, 8)
        pltpu.make_async_remote_copy(
            src_ref=parts.at[t], dst_ref=parts.at[t], send_sem=sx.at[0, 0], recv_sem=rx.at[t],
            device_id=(kv, tp), device_id_type=MESH,
        ).wait_recv()
        own += parts[t].astype(F32)
    own = jnp.where(core == 0, own[:, :576], own[:, 64:])
    square[...] = jnp.sum(
        jnp.where(row16 == lane16, jnp.sum(own * own, axis=1, keepdims=True), 0.0), axis=0, keepdims=True
    )

    def to_square(i):
        return pltpu.make_async_remote_copy(
            src_ref=square, dst_ref=squares.at[tp], send_sem=ss.at[i], recv_sem=rs.at[tp],
            device_id=(kv, lax.rem(tp + i, 8)), device_id_type=MESH,
        )

    for i in (4, 5, 3, 2, 6, 1, 7):
        to_square(i).start()
    resid = res_v[...].astype(F32)
    gained = own * gain_v[...].reshape(1, 576)
    sq = square[...]
    for i in range(1, 8):
        t = lax.rem(tp + i, 8)
        pltpu.make_async_remote_copy(
            src_ref=square, dst_ref=squares.at[t], send_sem=ss.at[0], recv_sem=rs.at[t],
            device_id=(kv, tp), device_id_type=MESH,
        ).wait_recv()
        sq += squares[t]
    sq = jnp.sum(jnp.where(row16 == lane16, sq, 0.0), axis=1, keepdims=True)
    scale = lax.rsqrt(sq / 4608.0 + 1e-06)
    o_ref[...] = (resid + gained * scale).astype(BF)

    for i in range(1, 8):
        to_holder(i).wait_send()
        along_row(i).wait_send()
        to_square(i).wait_send()
    for i in range(1, nx):
        to_group(i, 0).wait_send()
        to_group(i, 1).wait_send()
    to_group(0, 0).wait_send()

    sent = msgs.at[pl.ds(0, nz * ny - 1)]
    pltpu.make_async_copy(sent, sent, sr).wait()


def local(q, ids, kv, scales, suf, lens, w, res, gain):
    nz = ny = 8
    nx = lax.axis_size("tp") // 2
    hbm = pl.BlockSpec(memory_space=pl.ANY)
    vmem = pl.BlockSpec(memory_space=pltpu.VMEM)
    dma = pltpu.SemaphoreType.DMA

    def body(*refs):
        kernel(nz, ny, nx, *refs)

    return pl.pallas_call(
        body,
        out_shape=jax.ShapeDtypeStruct(res.shape, BF),
        in_specs=[hbm] * 9,
        out_specs=vmem,
        scratch_shapes=[
            pltpu.VMEM((16, 256), BF),
            pltpu.VMEM((1, 16), jnp.int32),
            pltpu.VMEM((1, 16), jnp.int32),
            pltpu.VMEM((2, 2048, 128), BF),
            pltpu.VMEM((2, 1, 2048), F32),
            pltpu.VMEM((2, 16, 128, 128), BF),
            pltpu.VMEM((256, 4608), BF),
            pltpu.VMEM((16, 576), BF),
            pltpu.VMEM((576,), F32),
            pltpu.VMEM((8, 16, 128), BF),
            pltpu.VMEM((8, 16, 128), BF),
            pltpu.VMEM((8, 96, 128), BF),
            pltpu.VMEM((64, 16, 128), BF),
            pltpu.VMEM((8, 8, 16, 128), BF),
            pltpu.VMEM((4, 2, 16, 640), BF),
            pltpu.VMEM((8, 16, 640), BF),
            pltpu.VMEM((1, 128), F32),
            pltpu.VMEM((8, 1, 128), F32),
            pltpu.VMEM((16, 576), BF),
            dma((9,)),
            pltpu.SemaphoreType.REGULAR,
            pltpu.SemaphoreType.REGULAR,
            dma((8,)), dma, dma((8,)), dma((8,)),
            dma, dma,
            dma((4, 2)), dma((8,)), dma((8,)), dma((8,)),
        ],
        compiler_params=pltpu.CompilerParams(
            collective_id=0, has_side_effects=True, vmem_limit_bytes=62 * 2**20
        ),
        cost_estimate=pl.CostEstimate(flops=10**9, bytes_accessed=5 * 10**6, transcendentals=3 * 10**6),
        name="attend",
    )(q, ids.reshape(1, 16), kv, scales, suf, lens.reshape(1, 16), w, res, gain)


def solution(mesh):
    placed = (
        P("kv", "tp"), P("kv", None), P(None, "kv", "tp"), P(None, "tp", "kv"), P(None, "kv", None, "tp"),
        P("kv"), P("tp", None), P("kv", "tp"), P("tp"),
    )
    return jax.shard_map(local, mesh=mesh, in_specs=placed, out_specs=P("kv", "tp"), check_vma=False)
```

```python
import jax
import jax.numpy as jnp
from jax import lax
from jax.experimental import pallas as pl
from jax.experimental.pallas import tpu as pltpu
from jax.sharding import PartitionSpec as P

HD = 128
NPRE = 8
SLOTS = 6
SLAB = 16
MESH = pl.DeviceIdType.MESH
BF = jnp.bfloat16
F32 = jnp.float32
LOG2E = 1.4426950408889634
SCORE = 144.0 ** (-0.5)
CHUNK = 256


def iota(shape, dim):
    return lax.broadcasted_iota(jnp.int32, shape, dim)


def nt(a, b):
    return lax.dot_general(a, b, (((1,), (1,)), ((), ())), preferred_element_type=F32)


def mm(a, b):
    return jnp.dot(a, b, preferred_element_type=F32)


def split(a):
    high = a.astype(BF)
    return high, (a - high.astype(F32)).astype(BF)


def kernel(
    nz, ny, nx,
    q_ref, ids_ref, kv_ref, scales_ref, suf_ref, len_ref, w_ref, res_ref, gain_ref,
    o_ref,
    q_v, ids_v, len_v, kv_v, sc_v, suf_v, w_v, res_v, gain_v,
    slots, gathered, blocks, msgs, back, part, parts, square, squares, out_v,
    local_sem, go_y, go_z, sy, ry, sz, rz, sr, rr, sx, rx, ss, rs,
):
    kv, tp = lax.axis_index("kv"), lax.axis_index("tp")
    y, z = lax.div(kv, nz), lax.rem(kv, nz)
    x, core = lax.div(tp, 2), lax.rem(tp, 2)

    barrier = pltpu.get_barrier_semaphore()

    def here(to_kv, to_tp):
        pl.semaphore_signal(barrier, inc=1, device_id=(to_kv, to_tp), device_id_type=MESH)

    late = nz // 2
    here(kv, x * 2 + (1 - core))
    for i in (4, 3, 5, 2, 6, 1, 7):
        here(lax.rem(y + i, ny) * nz + z, x * 2)
    for i in (4, 3, 5, 2, 6, 1, 7):
        here(y * nz + lax.rem(z + i, nz), x * 2 + jnp.where(z < late, 0, 1))
    for i in (2, 1, 3):
        here(kv, lax.rem(x + i, nx) * 2 + 1)

    def fetch(i, src, dst):
        c = pltpu.make_async_copy(src, dst, local_sem.at[i])
        c.start()
        return c

    got_q = fetch(0, q_ref, q_v)
    got_ids = fetch(7, ids_ref, ids_v)
    got_len = fetch(8, len_ref, len_v)
    got_kv = fetch(1, kv_ref, kv_v)
    got_sc = fetch(2, scales_ref, sc_v)
    got_suf = fetch(3, suf_ref, suf_v)
    got_w = fetch(4, w_ref, w_v)
    got_res = fetch(5, res_ref, res_v)
    got_gain = fetch(6, gain_ref, gain_v)

    row16, lane16 = iota((16, 128), 0), iota((16, 128), 1)
    got_ids.wait()
    ids_row = ids_v[...].astype(F32)
    square16 = iota((16, 16), 0), iota((16, 16), 1)
    ids = jnp.sum(jnp.where(square16[0] == square16[1], ids_row, 0.0), axis=1, keepdims=True)
    same = jnp.where(ids == ids_row, 1.0, 0.0)
    rank = jnp.sum(jnp.where(square16[1] < square16[0], same, 0.0), axis=1, keepdims=True)
    rank_row = jnp.sum(jnp.where(square16[0] < square16[1], same, 0.0), axis=0, keepdims=True)
    place = (ids * SLAB + rank).astype(jnp.int32)
    place_row = (ids_row * SLAB + rank_row).astype(jnp.int32)

    got_q.wait()
    row128 = iota((128, 16), 0)
    picks = [jnp.where(row128 == place_row + h * SLOTS, 1.0, 0.0).astype(BF) for h in range(2)]
    slotted = mm(picks[0], q_v[:, :HD]) + mm(picks[1], q_v[:, HD:])
    slots[...] = slotted.astype(BF).reshape(NPRE, SLAB, HD)

    @pl.when(core == 0)
    def _():
        pl.semaphore_wait(barrier, 1 + 2 * (ny - 1) + 2 * jnp.where(z < late, late - 1, late))
        pl.semaphore_signal(go_y, inc=1, device_id=(kv, tp + 1), device_id_type=MESH)

    @pl.when(core == 1)
    def _():
        pl.semaphore_wait(go_y, 1)

    def to_holder(i):
        p = lax.rem(y + i, ny)
        return pltpu.make_async_remote_copy(
            src_ref=slots.at[p], dst_ref=gathered.at[y], send_sem=sy.at[i], recv_sem=ry,
            device_id=(p * nz + z, tp), device_id_type=MESH,
        )

    for i in (4, 3, 5, 2, 6, 1, 7):
        to_holder(i).start()
    pltpu.make_async_copy(slots.at[y], gathered.at[y], ry).start()

    got_suf.wait()
    got_len.wait()
    eye = jnp.where(iota((32, 16), 1) == lax.rem(iota((32, 16), 0), 16), 1.0, 0.0)
    lens = jnp.sum(eye * len_v[...].astype(F32), axis=1, keepdims=True).astype(jnp.int32)
    own_q = jnp.concatenate([q_v[:, :HD], q_v[:, HD:]], axis=0)
    own_request = lax.rem(iota((32, CHUNK), 0), 16)
    suf_out = jnp.zeros((32, HD), F32)
    suf_total = jnp.zeros((32, 128), F32)
    for c in range(8):
        k = suf_v[0, 2 * c : 2 * c + 2].reshape(CHUNK, HD)
        v = suf_v[1, 2 * c : 2 * c + 2].reshape(CHUNK, HD)
        e = jnp.exp2(jnp.tanh(nt(own_q, k) * (SCORE / 50.0)) * (50.0 * LOG2E))
        at = iota((32, CHUNK), 1)
        live = (lax.div(at, 128) + 2 * c == own_request) & (lax.rem(at, 128) < lens)
        e = jnp.where(live, e, 0.0)
        suf_total += e[:, :128] + e[:, 128:]
        suf_out += mm(e.astype(BF), v)
    suf_total = jnp.sum(suf_total, axis=1, keepdims=True)

    got_kv.wait()
    got_sc.wait()
    sc_v[0] = sc_v[0] * (SCORE / 50.0)

    pltpu.make_async_copy(gathered, gathered, ry).wait()
    compact = jnp.where(
        iota((96, 128), 1) == lax.div(iota((96, 128), 0), 12) * SLAB + lax.rem(iota((96, 128), 0), 12), 1.0, 0.0
    ).astype(BF)
    blocks[z] = mm(compact, gathered[...].reshape(128, HD)).astype(BF)

    def along_row(i):
        return pltpu.make_async_remote_copy(
            src_ref=blocks.at[z], dst_ref=blocks.at[z], send_sem=sz.at[i], recv_sem=rz.at[z],
            device_id=(y * nz + lax.rem(z + i, nz), tp), device_id_type=MESH,
        )

    def to_half(half):
        for i in (4, 3, 5, 2, 6, 1, 7):

            @pl.when(lax.div(lax.rem(z + i, nz), late) == half)
            def _():
                along_row(i).start()

    to_half(0)

    expand = jnp.where(
        (iota((128, 96), 1) == lax.div(iota((128, 96), 0), SLAB) * 12 + lax.rem(iota((128, 96), 0), SLAB))
        & (lax.rem(iota((128, 96), 0), SLAB) < 12),
        1.0, 0.0,
    ).astype(BF)
    ones = jnp.ones((16, 128), BF)
    zeros = jnp.zeros((16, 32), F32)

    def row_of_totals(a):
        return jnp.concatenate([nt(ones, a), zeros], axis=1)

    in_slab = lax.rem(iota((128, 128), 0), SLAB)

    def back_to(b, i):
        to_y = lax.rem(y + i, ny)
        return pltpu.make_async_remote_copy(
            src_ref=msgs.at[b * ny + to_y], dst_ref=back.at[z, y], send_sem=sr, recv_sem=rr,
            device_id=(to_y * nz + b, tp), device_id_type=MESH,
        )

    def one_block(step, carry):
        @pl.when(step == jnp.where(z < late, jnp.where(z == 2, 2, 1), 0))
        def _():
            @pl.when(core == 1)
            def _():
                pl.semaphore_wait(barrier, 1 + 2 * (nx - 1) + 2 * jnp.where(z < late, late, late - 1))
                pl.semaphore_signal(go_z, inc=1, device_id=(kv, tp - 1), device_id_type=MESH)

            @pl.when(core == 0)
            def _():
                pl.semaphore_wait(go_z, 1)

            to_half(1)

        b = jnp.where((z >= late) | (step > z), step, jnp.where(step == 0, z, step - 1))

        @pl.when(b != z)
        def _():
            pltpu.make_async_remote_copy(
                src_ref=blocks.at[b], dst_ref=blocks.at[b], send_sem=sz.at[0], recv_sem=rz.at[b],
                device_id=(kv, tp), device_id_type=MESH,
            ).wait_recv()

        q = blocks[b]
        total = jnp.zeros((96, 128), F32)
        out = jnp.zeros((96, HD), F32)
        e = jnp.exp2(jnp.tanh(nt(q, kv_v[0]) * sc_v[0]) * (50.0 * LOG2E))
        for c in range(16):
            total += e[:, c * 128 : (c + 1) * 128]
        out += mm((e * sc_v[1]).astype(BF), kv_v[1])
        high, low = split(total)
        high, low = split(row_of_totals(high) + row_of_totals(low))
        msg = mm(expand, out.astype(BF))
        msg = jnp.where(in_slab == 12, high[:1].astype(F32), jnp.where(in_slab == 13, low[:1].astype(F32), msg))
        msgs[pl.ds(b * ny, ny)] = msg.astype(BF).reshape(NPRE, SLAB, HD)
        for i in (4, 3, 5, 2, 6, 1, 7):
            back_to(b, i).start()

        @pl.when(b != z)
        def _():
            back_to(b, 0).start()

        @pl.when(b == z)
        def _():
            pltpu.make_async_copy(msgs.at[z * ny + y], back.at[z, y], rr).start()

        return carry

    lax.fori_loop(0, nz, one_block, 0)

    lane = iota((16, 256), 1) & 127
    first = (ids * SLAB).astype(jnp.int32)
    picks = [jnp.where(lane == place + h * SLOTS, 1.0, 0.0) for h in range(2)]
    pick_total = jnp.where((lane == first + 12) | (lane == first + 13), 1.0, 0.0)
    picks = jnp.concatenate([picks[0], picks[1], pick_total], axis=0).astype(BF)
    pltpu.make_async_copy(back, back, rr).wait()
    summed = back[0].astype(F32)
    for a in range(1, 8):
        summed += back[a].astype(F32)
    high, low = split(summed.reshape(128, HD))
    held = jnp.concatenate([high, low], axis=0)
    found = mm(picks, held)
    total_rows = found[32:]
    rank_lane = y * 12 + rank.astype(jnp.int32)
    total = jnp.concatenate(
        [
            jnp.sum(jnp.where(lane16 == rank_lane + h * SLOTS, total_rows, 0.0), axis=1, keepdims=True)
            for h in range(2)
        ],
        axis=0,
    )
    att = ((found[:32] + suf_out) / (total + suf_total)).astype(BF)
    att = jnp.concatenate([att[:16], att[16:]], axis=1)

    got_w.wait()

    def to_group(i, c):
        return pltpu.make_async_remote_copy(
            src_ref=part.at[i, c], dst_ref=parts.at[tp], send_sem=sx.at[i, c], recv_sem=rx.at[tp],
            device_id=(kv, lax.rem(x + i, nx) * 2 + c), device_id_type=MESH,
        )

    for i in (2, 1, 3, 0):
        at = pl.multiple_of(lax.rem(x + i, nx) * 1152, 128)
        got = mm(att, w_v[:, pl.ds(at, 1152)])
        part[i, 0] = got[:, :640].astype(BF)
        part[i, 1] = got[:, 512:].astype(BF)
        if i:
            to_group(i, 0).start()
            to_group(i, 1).start()
        else:
            own = jnp.where(core == 0, got[:, :640], got[:, 512:])
            pltpu.make_async_remote_copy(
                src_ref=part.at[0, 1 - core], dst_ref=parts.at[tp], send_sem=sx.at[0, 0], recv_sem=rx.at[tp],
                device_id=(kv, x * 2 + (1 - core)), device_id_type=MESH,
            ).start()
    got_res.wait()
    got_gain.wait()
    for i in range(1, 8):
        t = lax.rem(tp + i, 8)
        pltpu.make_async_remote_copy(
            src_ref=parts.at[t], dst_ref=parts.at[t], send_sem=sx.at[0, 0], recv_sem=rx.at[t],
            device_id=(kv, tp), device_id_type=MESH,
        ).wait_recv()
        own += parts[t].astype(F32)
    own = jnp.where(core == 0, own[:, :576], own[:, 64:])
    square[...] = jnp.sum(
        jnp.where(row16 == lane16, jnp.sum(own * own, axis=1, keepdims=True), 0.0), axis=0, keepdims=True
    )

    def to_square(i):
        return pltpu.make_async_remote_copy(
            src_ref=square, dst_ref=squares.at[tp], send_sem=ss.at[i], recv_sem=rs.at[tp],
            device_id=(kv, lax.rem(tp + i, 8)), device_id_type=MESH,
        )

    for i in (4, 5, 3, 2, 6, 1, 7):
        to_square(i).start()
    resid = res_v[...].astype(F32)
    gained = own * gain_v[...].reshape(1, 576)
    for i in range(1, 8):
        to_holder(i).wait_send()
        along_row(i).wait_send()
        to_square(i).wait_send()
    for i in range(1, nx):
        to_group(i, 0).wait_send()
        to_group(i, 1).wait_send()
    to_group(0, 0).wait_send()

    sent = msgs.at[pl.ds(0, nz * ny - 1)]
    pltpu.make_async_copy(sent, sent, sr).wait()

    sq = square[...]
    for i in range(1, 8):
        t = lax.rem(tp + i, 8)
        pltpu.make_async_remote_copy(
            src_ref=square, dst_ref=squares.at[t], send_sem=ss.at[0], recv_sem=rs.at[t],
            device_id=(kv, tp), device_id_type=MESH,
        ).wait_recv()
        sq += squares[t]
    sq = jnp.sum(jnp.where(row16 == lane16, sq, 0.0), axis=1, keepdims=True)
    scale = lax.rsqrt(sq / 4608.0 + 1e-06)
    o_ref[...] = (resid + gained * scale).astype(BF)


def local(q, ids, kv, scales, suf, lens, w, res, gain):
    nz = ny = 8
    nx = lax.axis_size("tp") // 2
    hbm = pl.BlockSpec(memory_space=pl.ANY)
    vmem = pl.BlockSpec(memory_space=pltpu.VMEM)
    dma = pltpu.SemaphoreType.DMA

    def body(*refs):
        kernel(nz, ny, nx, *refs)

    return pl.pallas_call(
        body,
        out_shape=pltpu.VMEM(res.shape, BF),
        in_specs=[hbm] * 9,
        out_specs=vmem,
        scratch_shapes=[
            pltpu.VMEM((16, 256), BF),
            pltpu.VMEM((1, 16), jnp.int32),
            pltpu.VMEM((1, 16), jnp.int32),
            pltpu.VMEM((2, 2048, 128), BF),
            pltpu.VMEM((2, 1, 2048), F32),
            pltpu.VMEM((2, 16, 128, 128), BF),
            pltpu.VMEM((256, 4608), BF),
            pltpu.VMEM((16, 576), BF),
            pltpu.VMEM((576,), F32),
            pltpu.VMEM((8, 16, 128), BF),
            pltpu.VMEM((8, 16, 128), BF),
            pltpu.VMEM((8, 96, 128), BF),
            pltpu.VMEM((64, 16, 128), BF),
            pltpu.VMEM((8, 8, 16, 128), BF),
            pltpu.VMEM((4, 2, 16, 640), BF),
            pltpu.VMEM((8, 16, 640), BF),
            pltpu.VMEM((1, 128), F32),
            pltpu.VMEM((8, 1, 128), F32),
            pltpu.VMEM((16, 576), BF),
            dma((9,)),
            pltpu.SemaphoreType.REGULAR,
            pltpu.SemaphoreType.REGULAR,
            dma((8,)), dma, dma((8,)), dma((8,)),
            dma, dma,
            dma((4, 2)), dma((8,)), dma((8,)), dma((8,)),
        ],
        compiler_params=pltpu.CompilerParams(
            collective_id=0, has_side_effects=True, vmem_limit_bytes=62 * 2**20
        ),
        cost_estimate=pl.CostEstimate(flops=10**9, bytes_accessed=5 * 10**6, transcendentals=3 * 10**6),
        name="attend",
    )(q, ids.reshape(1, 16), kv, scales, suf, lens.reshape(1, 16), w, res, gain)


def solution(mesh):
    placed = (
        P("kv", "tp"), P("kv", None), P(None, "kv", "tp"), P(None, "tp", "kv"), P(None, "kv", None, "tp"),
        P("kv"), P("tp", None), P("kv", "tp"), P("tp"),
    )
    return jax.shard_map(local, mesh=mesh, in_specs=placed, out_specs=P("kv", "tp"), check_vma=False)
```

```python
import jax
import jax.numpy as jnp
from jax import lax
from jax.experimental import pallas as pl
from jax.experimental.pallas import tpu as pltpu
from jax.sharding import PartitionSpec as P

HD = 128
NPRE = 8
SLOTS = 6
SLAB = 16
MESH = pl.DeviceIdType.MESH
BF = jnp.bfloat16
F32 = jnp.float32
LOG2E = 1.4426950408889634
SCORE = 144.0 ** (-0.5)
CHUNK = 256


def iota(shape, dim):
    return lax.broadcasted_iota(jnp.int32, shape, dim)


def nt(a, b):
    return lax.dot_general(a, b, (((1,), (1,)), ((), ())), preferred_element_type=F32)


def mm(a, b):
    return jnp.dot(a, b, preferred_element_type=F32)


def split(a):
    high = a.astype(BF)
    return high, (a - high.astype(F32)).astype(BF)


def kernel(
    nz, ny, nx,
    q_ref, ids_ref, kv_ref, scales_ref, suf_ref, len_ref, w_ref, res_ref, gain_ref,
    o_ref,
    q_v, ids_v, len_v, kv_v, sc_v, suf_v, w_v, res_v, gain_v,
    slots, gathered, blocks, msgs, back, part, parts, square, squares, out_v,
    local_sem, go_y, go_z, sy, ry, sz, rz, sr, rr, sx, rx, ss, rs,
):
    kv, tp = lax.axis_index("kv"), lax.axis_index("tp")
    y, z = lax.div(kv, nz), lax.rem(kv, nz)
    x, core = lax.div(tp, 2), lax.rem(tp, 2)

    barrier = pltpu.get_barrier_semaphore()

    def here(to_kv, to_tp):
        pl.semaphore_signal(barrier, inc=1, device_id=(to_kv, to_tp), device_id_type=MESH)

    late = nz // 2
    here(kv, x * 2 + (1 - core))
    for i in (4, 3, 5, 2, 6, 1, 7):
        here(lax.rem(y + i, ny) * nz + z, x * 2)
    for i in (4, 3, 5, 2, 6, 1, 7):
        here(y * nz + lax.rem(z + i, nz), x * 2 + jnp.where(z < late, 0, 1))
    for i in (2, 1, 3):
        here(kv, lax.rem(x + i, nx) * 2 + 1)

    def fetch(i, src, dst):
        c = pltpu.make_async_copy(src, dst, local_sem.at[i])
        c.start()
        return c

    got_q = fetch(0, q_ref, q_v)
    got_ids = fetch(7, ids_ref, ids_v)
    got_len = fetch(8, len_ref, len_v)
    got_kv = fetch(1, kv_ref, kv_v)
    got_sc = fetch(2, scales_ref, sc_v)
    got_suf = fetch(3, suf_ref, suf_v)
    got_w = fetch(4, w_ref, w_v)
    got_res = fetch(5, res_ref, res_v)
    got_gain = fetch(6, gain_ref, gain_v)

    row16, lane16 = iota((16, 128), 0), iota((16, 128), 1)
    got_ids.wait()
    ids_row = ids_v[...].astype(F32)
    square16 = iota((16, 16), 0), iota((16, 16), 1)
    ids = jnp.sum(jnp.where(square16[0] == square16[1], ids_row, 0.0), axis=1, keepdims=True)
    same = jnp.where(ids == ids_row, 1.0, 0.0)
    rank = jnp.sum(jnp.where(square16[1] < square16[0], same, 0.0), axis=1, keepdims=True)
    rank_row = jnp.sum(jnp.where(square16[0] < square16[1], same, 0.0), axis=0, keepdims=True)
    place = (ids * SLAB + rank).astype(jnp.int32)
    place_row = (ids_row * SLAB + rank_row).astype(jnp.int32)

    got_q.wait()
    row128 = iota((128, 16), 0)
    picks = [jnp.where(row128 == place_row + h * SLOTS, 1.0, 0.0).astype(BF) for h in range(2)]
    slotted = mm(picks[0], q_v[:, :HD]) + mm(picks[1], q_v[:, HD:])
    slots[...] = slotted.astype(BF).reshape(NPRE, SLAB, HD)

    @pl.when(core == 0)
    def _():
        pl.semaphore_wait(barrier, 1 + 2 * (ny - 1) + 2 * jnp.where(z < late, late - 1, late))
        pl.semaphore_signal(go_y, inc=1, device_id=(kv, tp + 1), device_id_type=MESH)

    @pl.when(core == 1)
    def _():
        pl.semaphore_wait(go_y, 1)

    def to_holder(i):
        p = lax.rem(y + i, ny)
        return pltpu.make_async_remote_copy(
            src_ref=slots.at[p], dst_ref=gathered.at[y], send_sem=sy.at[i], recv_sem=ry,
            device_id=(p * nz + z, tp), device_id_type=MESH,
        )

    for i in (4, 3, 5, 2, 6, 1, 7):
        to_holder(i).start()
    pltpu.make_async_copy(slots.at[y], gathered.at[y], ry).start()

    got_suf.wait()
    got_len.wait()
    eye = jnp.where(iota((32, 16), 1) == lax.rem(iota((32, 16), 0), 16), 1.0, 0.0)
    lens = jnp.sum(eye * len_v[...].astype(F32), axis=1, keepdims=True).astype(jnp.int32)
    own_q = jnp.concatenate([q_v[:, :HD], q_v[:, HD:]], axis=0)
    own_request = lax.rem(iota((32, CHUNK), 0), 16)
    suf_out = jnp.zeros((32, HD), F32)
    suf_total = jnp.zeros((32, 128), F32)
    for c in range(8):
        k = suf_v[0, 2 * c : 2 * c + 2].reshape(CHUNK, HD)
        v = suf_v[1, 2 * c : 2 * c + 2].reshape(CHUNK, HD)
        e = jnp.exp2(jnp.tanh(nt(own_q, k) * (SCORE / 50.0)) * (50.0 * LOG2E))
        at = iota((32, CHUNK), 1)
        live = (lax.div(at, 128) + 2 * c == own_request) & (lax.rem(at, 128) < lens)
        e = jnp.where(live, e, 0.0)
        suf_total += e[:, :128] + e[:, 128:]
        suf_out += mm(e.astype(BF), v)
    suf_total = jnp.sum(suf_total, axis=1, keepdims=True)

    got_kv.wait()
    got_sc.wait()
    sc_v[0] = sc_v[0] * (SCORE / 50.0)

    pltpu.make_async_copy(gathered, gathered, ry).wait()
    compact = jnp.where(
        iota((96, 128), 1) == lax.div(iota((96, 128), 0), 12) * SLAB + lax.rem(iota((96, 128), 0), 12), 1.0, 0.0
    ).astype(BF)
    blocks[z] = mm(compact, gathered[...].reshape(128, HD)).astype(BF)

    def along_row(i):
        return pltpu.make_async_remote_copy(
            src_ref=blocks.at[z], dst_ref=blocks.at[z], send_sem=sz.at[i], recv_sem=rz.at[z],
            device_id=(y * nz + lax.rem(z + i, nz), tp), device_id_type=MESH,
        )

    def to_half(half):
        for i in (4, 3, 5, 2, 6, 1, 7):

            @pl.when(lax.div(lax.rem(z + i, nz), late) == half)
            def _():
                along_row(i).start()

    to_half(0)

    expand = jnp.where(
        (iota((128, 96), 1) == lax.div(iota((128, 96), 0), SLAB) * 12 + lax.rem(iota((128, 96), 0), SLAB))
        & (lax.rem(iota((128, 96), 0), SLAB) < 12),
        1.0, 0.0,
    ).astype(BF)
    ones = jnp.ones((16, 128), BF)
    zeros = jnp.zeros((16, 32), F32)

    def row_of_totals(a):
        return jnp.concatenate([nt(ones, a), zeros], axis=1)

    in_slab = lax.rem(iota((128, 128), 0), SLAB)

    def back_to(b, i):
        to_y = lax.rem(y + i, ny)
        return pltpu.make_async_remote_copy(
            src_ref=msgs.at[b * ny + to_y], dst_ref=back.at[z, y], send_sem=sr, recv_sem=rr,
            device_id=(to_y * nz + b, tp), device_id_type=MESH,
        )

    def one_block(step, carry):
        @pl.when(step == jnp.where(z < late, jnp.where(z == 2, 2, 1), 0))
        def _():
            @pl.when(core == 1)
            def _():
                pl.semaphore_wait(barrier, 1 + 2 * (nx - 1) + 2 * jnp.where(z < late, late, late - 1))
                pl.semaphore_signal(go_z, inc=1, device_id=(kv, tp - 1), device_id_type=MESH)

            @pl.when(core == 0)
            def _():
                pl.semaphore_wait(go_z, 1)

            to_half(1)

        b = jnp.where(z < late, jnp.where(step > z, step, jnp.where(step == 0, z, step - 1)), jnp.where(step == 1, 2, jnp.where(step == 2, 1, step)))

        @pl.when(b != z)
        def _():
            pltpu.make_async_remote_copy(
                src_ref=blocks.at[b], dst_ref=blocks.at[b], send_sem=sz.at[0], recv_sem=rz.at[b],
                device_id=(kv, tp), device_id_type=MESH,
            ).wait_recv()

        q = blocks[b]
        total = jnp.zeros((96, 128), F32)
        out = jnp.zeros((96, HD), F32)
        e = jnp.exp2(jnp.tanh(nt(q, kv_v[0]) * sc_v[0]) * (50.0 * LOG2E))
        for c in range(16):
            total += e[:, c * 128 : (c + 1) * 128]
        out += mm((e * sc_v[1]).astype(BF), kv_v[1])
        high, low = split(total)
        high, low = split(row_of_totals(high) + row_of_totals(low))
        msg = mm(expand, out.astype(BF))
        msg = jnp.where(in_slab == 12, high[:1].astype(F32), jnp.where(in_slab == 13, low[:1].astype(F32), msg))
        msgs[pl.ds(b * ny, ny)] = msg.astype(BF).reshape(NPRE, SLAB, HD)
        for i in (4, 3, 5, 2, 6, 1, 7):
            back_to(b, i).start()

        @pl.when(b != z)
        def _():
            back_to(b, 0).start()

        @pl.when(b == z)
        def _():
            pltpu.make_async_copy(msgs.at[z * ny + y], back.at[z, y], rr).start()

        return carry

    lax.fori_loop(0, nz, one_block, 0)

    lane = iota((16, 256), 1) & 127
    first = (ids * SLAB).astype(jnp.int32)
    picks = [jnp.where(lane == place + h * SLOTS, 1.0, 0.0) for h in range(2)]
    pick_total = jnp.where((lane == first + 12) | (lane == first + 13), 1.0, 0.0)
    picks = jnp.concatenate([picks[0], picks[1], pick_total], axis=0).astype(BF)
    pltpu.make_async_copy(back, back, rr).wait()
    summed = back[0].astype(F32)
    for a in range(1, 8):
        summed += back[a].astype(F32)
    high, low = split(summed.reshape(128, HD))
    held = jnp.concatenate([high, low], axis=0)
    found = mm(picks, held)
    total_rows = found[32:]
    rank_lane = y * 12 + rank.astype(jnp.int32)
    total = jnp.concatenate(
        [
            jnp.sum(jnp.where(lane16 == rank_lane + h * SLOTS, total_rows, 0.0), axis=1, keepdims=True)
            for h in range(2)
        ],
        axis=0,
    )
    att = ((found[:32] + suf_out) / (total + suf_total)).astype(BF)
    att = jnp.concatenate([att[:16], att[16:]], axis=1)

    got_w.wait()

    def to_group(i, c):
        return pltpu.make_async_remote_copy(
            src_ref=part.at[i, c], dst_ref=parts.at[tp], send_sem=sx.at[i, c], recv_sem=rx.at[tp],
            device_id=(kv, lax.rem(x + i, nx) * 2 + c), device_id_type=MESH,
        )

    for i in (2, 1, 3, 0):
        at = pl.multiple_of(lax.rem(x + i, nx) * 1152, 128)
        got = mm(att, w_v[:, pl.ds(at, 1152)])
        part[i, 0] = got[:, :640].astype(BF)
        part[i, 1] = got[:, 512:].astype(BF)
        if i:
            to_group(i, 0).start()
            to_group(i, 1).start()
        else:
            own = jnp.where(core == 0, got[:, :640], got[:, 512:])
            pltpu.make_async_remote_copy(
                src_ref=part.at[0, 1 - core], dst_ref=parts.at[tp], send_sem=sx.at[0, 0], recv_sem=rx.at[tp],
                device_id=(kv, x * 2 + (1 - core)), device_id_type=MESH,
            ).start()
    got_res.wait()
    got_gain.wait()
    for i in range(1, 8):
        t = lax.rem(tp + i, 8)
        pltpu.make_async_remote_copy(
            src_ref=parts.at[t], dst_ref=parts.at[t], send_sem=sx.at[0, 0], recv_sem=rx.at[t],
            device_id=(kv, tp), device_id_type=MESH,
        ).wait_recv()
        own += parts[t].astype(F32)
    own = jnp.where(core == 0, own[:, :576], own[:, 64:])
    square[...] = jnp.sum(
        jnp.where(row16 == lane16, jnp.sum(own * own, axis=1, keepdims=True), 0.0), axis=0, keepdims=True
    )

    def to_square(i):
        return pltpu.make_async_remote_copy(
            src_ref=square, dst_ref=squares.at[tp], send_sem=ss.at[i], recv_sem=rs.at[tp],
            device_id=(kv, lax.rem(tp + i, 8)), device_id_type=MESH,
        )

    for i in (4, 5, 3, 2, 6, 1, 7):
        to_square(i).start()
    resid = res_v[...].astype(F32)
    gained = own * gain_v[...].reshape(1, 576)
    for i in range(1, 8):
        to_holder(i).wait_send()
        along_row(i).wait_send()
        to_square(i).wait_send()
    for i in range(1, nx):
        to_group(i, 0).wait_send()
        to_group(i, 1).wait_send()
    to_group(0, 0).wait_send()

    sent = msgs.at[pl.ds(0, nz * ny - 1)]
    pltpu.make_async_copy(sent, sent, sr).wait()

    sq = square[...]
    for i in range(1, 8):
        t = lax.rem(tp + i, 8)
        pltpu.make_async_remote_copy(
            src_ref=square, dst_ref=squares.at[t], send_sem=ss.at[0], recv_sem=rs.at[t],
            device_id=(kv, tp), device_id_type=MESH,
        ).wait_recv()
        sq += squares[t]
    sq = jnp.sum(jnp.where(row16 == lane16, sq, 0.0), axis=1, keepdims=True)
    scale = lax.rsqrt(sq / 4608.0 + 1e-06)
    o_ref[...] = (resid + gained * scale).astype(BF)


def local(q, ids, kv, scales, suf, lens, w, res, gain):
    nz = ny = 8
    nx = lax.axis_size("tp") // 2
    hbm = pl.BlockSpec(memory_space=pl.ANY)
    vmem = pl.BlockSpec(memory_space=pltpu.VMEM)
    dma = pltpu.SemaphoreType.DMA

    def body(*refs):
        kernel(nz, ny, nx, *refs)

    return pl.pallas_call(
        body,
        out_shape=pltpu.VMEM(res.shape, BF),
        in_specs=[hbm] * 9,
        out_specs=vmem,
        scratch_shapes=[
            pltpu.VMEM((16, 256), BF),
            pltpu.VMEM((1, 16), jnp.int32),
            pltpu.VMEM((1, 16), jnp.int32),
            pltpu.VMEM((2, 2048, 128), BF),
            pltpu.VMEM((2, 1, 2048), F32),
            pltpu.VMEM((2, 16, 128, 128), BF),
            pltpu.VMEM((256, 4608), BF),
            pltpu.VMEM((16, 576), BF),
            pltpu.VMEM((576,), F32),
            pltpu.VMEM((8, 16, 128), BF),
            pltpu.VMEM((8, 16, 128), BF),
            pltpu.VMEM((8, 96, 128), BF),
            pltpu.VMEM((64, 16, 128), BF),
            pltpu.VMEM((8, 8, 16, 128), BF),
            pltpu.VMEM((4, 2, 16, 640), BF),
            pltpu.VMEM((8, 16, 640), BF),
            pltpu.VMEM((1, 128), F32),
            pltpu.VMEM((8, 1, 128), F32),
            pltpu.VMEM((16, 576), BF),
            dma((9,)),
            pltpu.SemaphoreType.REGULAR,
            pltpu.SemaphoreType.REGULAR,
            dma((8,)), dma, dma((8,)), dma((8,)),
            dma, dma,
            dma((4, 2)), dma((8,)), dma((8,)), dma((8,)),
        ],
        compiler_params=pltpu.CompilerParams(
            collective_id=0, has_side_effects=True, vmem_limit_bytes=62 * 2**20
        ),
        cost_estimate=pl.CostEstimate(flops=10**9, bytes_accessed=5 * 10**6, transcendentals=3 * 10**6),
        name="attend",
    )(q, ids.reshape(1, 16), kv, scales, suf, lens.reshape(1, 16), w, res, gain)


def solution(mesh):
    placed = (
        P("kv", "tp"), P("kv", None), P(None, "kv", "tp"), P(None, "tp", "kv"), P(None, "kv", None, "tp"),
        P("kv"), P("tp", None), P("kv", "tp"), P("tp"),
    )
    return jax.shard_map(local, mesh=mesh, in_specs=placed, out_specs=P("kv", "tp"), check_vma=False)
```

```python
import jax
import jax.numpy as jnp
from jax import lax
from jax.experimental import pallas as pl
from jax.experimental.pallas import tpu as pltpu
from jax.sharding import PartitionSpec as P

HD = 128
NPRE = 8
SLOTS = 6
SLAB = 16
MESH = pl.DeviceIdType.MESH
BF = jnp.bfloat16
F32 = jnp.float32
LOG2E = 1.4426950408889634
SCORE = 144.0 ** (-0.5)
CHUNK = 256


def iota(shape, dim):
    return lax.broadcasted_iota(jnp.int32, shape, dim)


def nt(a, b):
    return lax.dot_general(a, b, (((1,), (1,)), ((), ())), preferred_element_type=F32)


def mm(a, b):
    return jnp.dot(a, b, preferred_element_type=F32)


def split(a):
    high = a.astype(BF)
    return high, (a - high.astype(F32)).astype(BF)


def kernel(
    nz, ny, nx,
    q_ref, ids_ref, kv_ref, scales_ref, suf_ref, len_ref, w_ref, res_ref, gain_ref,
    o_ref,
    q_v, ids_v, len_v, kv_v, sc_v, suf_v, w_v, res_v, gain_v,
    slots, gathered, blocks, msgs, back, part, parts, square, squares, out_v,
    local_sem, go_y, go_z, sy, ry, sz, rz, sr, rr, sx, rx, ss, rs,
):
    kv, tp = lax.axis_index("kv"), lax.axis_index("tp")
    y, z = lax.div(kv, nz), lax.rem(kv, nz)
    x, core = lax.div(tp, 2), lax.rem(tp, 2)

    barrier = pltpu.get_barrier_semaphore()

    def here(to_kv, to_tp):
        pl.semaphore_signal(barrier, inc=1, device_id=(to_kv, to_tp), device_id_type=MESH)

    late = nz // 2
    here(kv, x * 2 + (1 - core))
    for i in (4, 3, 5, 2, 6, 1, 7):
        here(lax.rem(y + i, ny) * nz + z, x * 2)
    for i in (4, 3, 5, 2, 6, 1, 7):
        here(y * nz + lax.rem(z + i, nz), x * 2 + jnp.where(z < late, 0, 1))
    for i in (2, 1, 3):
        here(kv, lax.rem(x + i, nx) * 2 + 1)

    def fetch(i, src, dst):
        c = pltpu.make_async_copy(src, dst, local_sem.at[i])
        c.start()
        return c

    got_q = fetch(0, q_ref, q_v)
    got_ids = fetch(7, ids_ref, ids_v)
    got_len = fetch(8, len_ref, len_v)
    got_kv = fetch(1, kv_ref, kv_v)
    got_sc = fetch(2, scales_ref, sc_v)
    got_suf = fetch(3, suf_ref, suf_v)
    got_w = fetch(4, w_ref, w_v)
    got_res = fetch(5, res_ref, res_v)
    got_gain = fetch(6, gain_ref, gain_v)

    row16, lane16 = iota((16, 128), 0), iota((16, 128), 1)
    got_ids.wait()
    ids_row = ids_v[...].astype(F32)
    square16 = iota((16, 16), 0), iota((16, 16), 1)
    ids = jnp.sum(jnp.where(square16[0] == square16[1], ids_row, 0.0), axis=1, keepdims=True)
    same = jnp.where(ids == ids_row, 1.0, 0.0)
    rank = jnp.sum(jnp.where(square16[1] < square16[0], same, 0.0), axis=1, keepdims=True)
    rank_row = jnp.sum(jnp.where(square16[0] < square16[1], same, 0.0), axis=0, keepdims=True)
    place = (ids * SLAB + rank).astype(jnp.int32)
    place_row = (ids_row * SLAB + rank_row).astype(jnp.int32)

    got_q.wait()
    row128 = iota((128, 16), 0)
    picks = [jnp.where(row128 == place_row + h * SLOTS, 1.0, 0.0).astype(BF) for h in range(2)]
    slotted = mm(picks[0], q_v[:, :HD]) + mm(picks[1], q_v[:, HD:])
    slots[...] = slotted.astype(BF).reshape(NPRE, SLAB, HD)

    @pl.when(core == 0)
    def _():
        pl.semaphore_wait(barrier, 1 + 2 * (ny - 1) + 2 * jnp.where(z < late, late - 1, late))
        pl.semaphore_signal(go_y, inc=1, device_id=(kv, tp + 1), device_id_type=MESH)

    @pl.when(core == 1)
    def _():
        pl.semaphore_wait(go_y, 1)

    def to_holder(i):
        p = lax.rem(y + i, ny)
        return pltpu.make_async_remote_copy(
            src_ref=slots.at[p], dst_ref=gathered.at[y], send_sem=sy.at[i], recv_sem=ry,
            device_id=(p * nz + z, tp), device_id_type=MESH,
        )

    for i in (4, 3, 5, 2, 6, 1, 7):
        to_holder(i).start()
    pltpu.make_async_copy(slots.at[y], gathered.at[y], ry).start()

    got_suf.wait()
    got_len.wait()
    eye = jnp.where(iota((32, 16), 1) == lax.rem(iota((32, 16), 0), 16), 1.0, 0.0)
    lens = jnp.sum(eye * len_v[...].astype(F32), axis=1, keepdims=True).astype(jnp.int32)
    own_q = jnp.concatenate([q_v[:, :HD], q_v[:, HD:]], axis=0)
    own_request = lax.rem(iota((32, CHUNK), 0), 16)
    suf_out = jnp.zeros((32, HD), F32)
    suf_total = jnp.zeros((32, 128), F32)
    for c in range(8):
        k = suf_v[0, 2 * c : 2 * c + 2].reshape(CHUNK, HD)
        v = suf_v[1, 2 * c : 2 * c + 2].reshape(CHUNK, HD)
        e = jnp.exp2(jnp.tanh(nt(own_q, k) * (SCORE / 50.0)) * (50.0 * LOG2E))
        at = iota((32, CHUNK), 1)
        live = (lax.div(at, 128) + 2 * c == own_request) & (lax.rem(at, 128) < lens)
        e = jnp.where(live, e, 0.0)
        suf_total += e[:, :128] + e[:, 128:]
        suf_out += mm(e.astype(BF), v)
    suf_total = jnp.sum(suf_total, axis=1, keepdims=True)

    got_kv.wait()
    got_sc.wait()
    sc_v[0] = sc_v[0] * (SCORE / 50.0)

    pltpu.make_async_copy(gathered, gathered, ry).wait()
    compact = jnp.where(
        iota((96, 128), 1) == lax.div(iota((96, 128), 0), 12) * SLAB + lax.rem(iota((96, 128), 0), 12), 1.0, 0.0
    ).astype(BF)
    blocks[z] = mm(compact, gathered[...].reshape(128, HD)).astype(BF)

    def along_row(i):
        return pltpu.make_async_remote_copy(
            src_ref=blocks.at[z], dst_ref=blocks.at[z], send_sem=sz.at[i], recv_sem=rz.at[z],
            device_id=(y * nz + lax.rem(z + i, nz), tp), device_id_type=MESH,
        )

    def to_half(half):
        for i in (4, 3, 5, 2, 6, 1, 7):

            @pl.when(lax.div(lax.rem(z + i, nz), late) == half)
            def _():
                along_row(i).start()

    to_half(0)

    expand = jnp.where(
        (iota((128, 96), 1) == lax.div(iota((128, 96), 0), SLAB) * 12 + lax.rem(iota((128, 96), 0), SLAB))
        & (lax.rem(iota((128, 96), 0), SLAB) < 12),
        1.0, 0.0,
    ).astype(BF)
    ones = jnp.ones((16, 128), BF)
    zeros = jnp.zeros((16, 32), F32)

    def row_of_totals(a):
        return jnp.concatenate([nt(ones, a), zeros], axis=1)

    in_slab = lax.rem(iota((128, 128), 0), SLAB)

    def back_to(b, i):
        to_y = lax.rem(y + i, ny)
        return pltpu.make_async_remote_copy(
            src_ref=msgs.at[b * ny + to_y], dst_ref=back.at[z, y], send_sem=sr, recv_sem=rr,
            device_id=(to_y * nz + b, tp), device_id_type=MESH,
        )

    def one_block(step, carry):
        @pl.when(step == jnp.where(z < late, jnp.where(z == 2, 2, 1), 0))
        def _():
            @pl.when(core == 1)
            def _():
                pl.semaphore_wait(barrier, 1 + 2 * (nx - 1) + 2 * jnp.where(z < late, late, late - 1))
                pl.semaphore_signal(go_z, inc=1, device_id=(kv, tp - 1), device_id_type=MESH)

            @pl.when(core == 0)
            def _():
                pl.semaphore_wait(go_z, 1)

            to_half(1)

        b = jnp.where(z < late, jnp.where(step > z, step, jnp.where(step == 0, z, step - 1)), jnp.where(step == 1, 2, jnp.where(step == 2, 1, step)))

        @pl.when(b != z)
        def _():
            pltpu.make_async_remote_copy(
                src_ref=blocks.at[b], dst_ref=blocks.at[b], send_sem=sz.at[0], recv_sem=rz.at[b],
                device_id=(kv, tp), device_id_type=MESH,
            ).wait_recv()

        q = blocks[b]
        total = jnp.zeros((96, 128), F32)
        out = jnp.zeros((96, HD), F32)
        e = jnp.exp2(jnp.tanh(nt(q, kv_v[0]) * sc_v[0]) * (50.0 * LOG2E))
        for c in range(16):
            total += e[:, c * 128 : (c + 1) * 128]
        out += mm((e * sc_v[1]).astype(BF), kv_v[1])
        high, low = split(total)
        high, low = split(row_of_totals(high) + row_of_totals(low))
        msg = mm(expand, out.astype(BF))
        msg = jnp.where(in_slab == 12, high[:1].astype(F32), jnp.where(in_slab == 13, low[:1].astype(F32), msg))
        msgs[pl.ds(b * ny, ny)] = msg.astype(BF).reshape(NPRE, SLAB, HD)
        for i in (4, 3, 5, 2, 6, 1, 7):
            back_to(b, i).start()

        @pl.when(b != z)
        def _():
            back_to(b, 0).start()

        @pl.when(b == z)
        def _():
            pltpu.make_async_copy(msgs.at[z * ny + y], back.at[z, y], rr).start()

        return carry

    lax.fori_loop(0, nz, one_block, 0)

    lane = iota((16, 8 * 128), 1) & 127
    first = (ids * SLAB).astype(jnp.int32)
    picks = [jnp.where(lane == place + h * SLOTS, 1.0, 0.0) for h in range(2)]
    pick_total = jnp.where((lane == first + 12) | (lane == first + 13), 1.0, 0.0)
    picks = jnp.concatenate([picks[0], picks[1], pick_total], axis=0).astype(BF)
    pltpu.make_async_copy(back, back, rr).wait()
    found = mm(picks, back[...].reshape(8 * 128, HD))
    total_rows = found[32:]
    rank_lane = y * 12 + rank.astype(jnp.int32)
    total = jnp.concatenate(
        [
            jnp.sum(jnp.where(lane16 == rank_lane + h * SLOTS, total_rows, 0.0), axis=1, keepdims=True)
            for h in range(2)
        ],
        axis=0,
    )
    att = ((found[:32] + suf_out) / (total + suf_total)).astype(BF)
    att = jnp.concatenate([att[:16], att[16:]], axis=1)

    got_w.wait()

    def to_group(i, c):
        return pltpu.make_async_remote_copy(
            src_ref=part.at[i, c], dst_ref=parts.at[tp], send_sem=sx.at[i, c], recv_sem=rx.at[tp],
            device_id=(kv, lax.rem(x + i, nx) * 2 + c), device_id_type=MESH,
        )

    for i in (2, 1, 3, 0):
        at = pl.multiple_of(lax.rem(x + i, nx) * 1152, 128)
        got = mm(att, w_v[:, pl.ds(at, 1152)])
        part[i, 0] = got[:, :640].astype(BF)
        part[i, 1] = got[:, 512:].astype(BF)
        if i:
            to_group(i, 0).start()
            to_group(i, 1).start()
        else:
            own = jnp.where(core == 0, got[:, :640], got[:, 512:])
            pltpu.make_async_remote_copy(
                src_ref=part.at[0, 1 - core], dst_ref=parts.at[tp], send_sem=sx.at[0, 0], recv_sem=rx.at[tp],
                device_id=(kv, x * 2 + (1 - core)), device_id_type=MESH,
            ).start()
    got_res.wait()
    got_gain.wait()
    for i in range(1, 8):
        t = lax.rem(tp + i, 8)
        pltpu.make_async_remote_copy(
            src_ref=parts.at[t], dst_ref=parts.at[t], send_sem=sx.at[0, 0], recv_sem=rx.at[t],
            device_id=(kv, tp), device_id_type=MESH,
        ).wait_recv()
        own += parts[t].astype(F32)
    own = jnp.where(core == 0, own[:, :576], own[:, 64:])
    square[...] = jnp.sum(
        jnp.where(row16 == lane16, jnp.sum(own * own, axis=1, keepdims=True), 0.0), axis=0, keepdims=True
    )

    def to_square(i):
        return pltpu.make_async_remote_copy(
            src_ref=square, dst_ref=squares.at[tp], send_sem=ss.at[i], recv_sem=rs.at[tp],
            device_id=(kv, lax.rem(tp + i, 8)), device_id_type=MESH,
        )

    for i in (4, 5, 3, 2, 6, 1, 7):
        to_square(i).start()
    resid = res_v[...].astype(F32)
    gained = own * gain_v[...].reshape(1, 576)
    for i in range(1, 8):
        to_holder(i).wait_send()
        along_row(i).wait_send()
        to_square(i).wait_send()
    for i in range(1, nx):
        to_group(i, 0).wait_send()
        to_group(i, 1).wait_send()
    to_group(0, 0).wait_send()

    sent = msgs.at[pl.ds(0, nz * ny - 1)]
    pltpu.make_async_copy(sent, sent, sr).wait()

    sq = square[...]
    for i in range(1, 8):
        t = lax.rem(tp + i, 8)
        pltpu.make_async_remote_copy(
            src_ref=square, dst_ref=squares.at[t], send_sem=ss.at[0], recv_sem=rs.at[t],
            device_id=(kv, tp), device_id_type=MESH,
        ).wait_recv()
        sq += squares[t]
    sq = jnp.sum(jnp.where(row16 == lane16, sq, 0.0), axis=1, keepdims=True)
    scale = lax.rsqrt(sq / 4608.0 + 1e-06)
    o_ref[...] = (resid + gained * scale).astype(BF)


def local(q, ids, kv, scales, suf, lens, w, res, gain):
    nz = ny = 8
    nx = lax.axis_size("tp") // 2
    hbm = pl.BlockSpec(memory_space=pl.ANY)
    vmem = pl.BlockSpec(memory_space=pltpu.VMEM)
    dma = pltpu.SemaphoreType.DMA

    def body(*refs):
        kernel(nz, ny, nx, *refs)

    return pl.pallas_call(
        body,
        out_shape=pltpu.VMEM(res.shape, BF),
        in_specs=[hbm] * 9,
        out_specs=vmem,
        scratch_shapes=[
            pltpu.VMEM((16, 256), BF),
            pltpu.VMEM((1, 16), jnp.int32),
            pltpu.VMEM((1, 16), jnp.int32),
            pltpu.VMEM((2, 2048, 128), BF),
            pltpu.VMEM((2, 1, 2048), F32),
            pltpu.VMEM((2, 16, 128, 128), BF),
            pltpu.VMEM((256, 4608), BF),
            pltpu.VMEM((16, 576), BF),
            pltpu.VMEM((576,), F32),
            pltpu.VMEM((8, 16, 128), BF),
            pltpu.VMEM((8, 16, 128), BF),
            pltpu.VMEM((8, 96, 128), BF),
            pltpu.VMEM((64, 16, 128), BF),
            pltpu.VMEM((8, 8, 16, 128), BF),
            pltpu.VMEM((4, 2, 16, 640), BF),
            pltpu.VMEM((8, 16, 640), BF),
            pltpu.VMEM((1, 128), F32),
            pltpu.VMEM((8, 1, 128), F32),
            pltpu.VMEM((16, 576), BF),
            dma((9,)),
            pltpu.SemaphoreType.REGULAR,
            pltpu.SemaphoreType.REGULAR,
            dma((8,)), dma, dma((8,)), dma((8,)),
            dma, dma,
            dma((4, 2)), dma((8,)), dma((8,)), dma((8,)),
        ],
        compiler_params=pltpu.CompilerParams(
            collective_id=0, has_side_effects=True, vmem_limit_bytes=62 * 2**20
        ),
        cost_estimate=pl.CostEstimate(flops=10**9, bytes_accessed=5 * 10**6, transcendentals=3 * 10**6),
        name="attend",
    )(q, ids.reshape(1, 16), kv, scales, suf, lens.reshape(1, 16), w, res, gain)


def solution(mesh):
    placed = (
        P("kv", "tp"), P("kv", None), P(None, "kv", "tp"), P(None, "tp", "kv"), P(None, "kv", None, "tp"),
        P("kv"), P("tp", None), P("kv", "tp"), P("tp"),
    )
    return jax.shard_map(local, mesh=mesh, in_specs=placed, out_specs=P("kv", "tp"), check_vma=False)
```
